256 devices in a mesh: dp: 16 (over x_lo, y, core), tensor: 16 (over z, x_hi).
Axes of the slice: x: 4 (x_hi: 2, x_lo: 2; x = x_hi * 2 + x_lo), y: 4, z: 8, core: 2. Of those that a mesh axis runs over, the one named last changes fastest.
Arguments:
- layer_input: bfloat16 [16384, 4096], P(('dp', 'tensor')), parts along dimension 0, may hold values from -6 to 10
- norm_gain: float32 [4096], replicated, may hold values from 0.25 to 1.75
- query_weight: bfloat16 [4096, 4096], P(None, 'tensor'), may hold values from -1 to 1
- key_weight: bfloat16 [4096, 1024], P(None, 'tensor'), may hold values from -1 to 1
- value_matrix: bfloat16 [4096, 1024], P(None, 'tensor'), may hold values from -0.09375 to 0.09375
- output_weight: bfloat16 [4096, 4096], P('tensor'), may hold values from -0.09375 to 0.09375
- keep_bits: int32 [512, 16, 16], P(('dp', 'tensor')), parts along dimension 0, may hold values 0 or 1
Outputs:
- layer_output: bfloat16 [16384, 4096], P(('dp', 'tensor')), parts along dimension 0
The draws below stay inside these ranges and needn't reach their ends.
There are 16 independent parts, one for each index of `dp`. The reference program is written for one: setup_inputs(seed, part) draws one part's arguments, and reference() takes and returns one part's arrays. A program takes and returns all parts, laid end to end along the dimension named above; an argument that names none is the same for every part. Nothing has to cross between parts.
All inputs are finite; a program needn't handle non-finite values. No bound on the sum of `keep_bits` on one device may be relied on, other than what follows from the above.
Results may differ from the reference program's by a relative error of at most 0.0095.
Values may be sent and summed in bfloat16 or wider, within the bound.
No kernel may reach another device: no remote copies, remote signals or barrier semaphores. Data moves between devices by JAX's collectives and lax.ppermute only.
A program may use at most 128 MiB of HBM per device.

```python
import math
import jax
import jax.numpy as jnp
from jax import lax

MODEL_WIDTH = 4096
QUERY_HEADS = 32
KEY_VALUE_HEADS = 8
HEAD_SIZE = 128
BLOCK = 64
LEN = 1024
NB = 16
N_TENSOR = 16


def draw_layer_input(key, part):
    rotary_base = jax.random.truncated_normal(jax.random.fold_in(key, 201), -6.0, 6.0, (LEN, MODEL_WIDTH), jnp.float32)
    return rotary_base.astype(jnp.bfloat16)


def draw_query_weight(key, part):
    rotary_base = jax.random.truncated_normal(jax.random.fold_in(key, 101), -4.0, 4.0, (MODEL_WIDTH, QUERY_HEADS * HEAD_SIZE), jnp.float32) / math.sqrt(MODEL_WIDTH)
    return rotary_base.astype(jnp.bfloat16)


def draw_key_weight(key, part):
    rotary_base = jax.random.truncated_normal(jax.random.fold_in(key, 102), -4.0, 4.0, (MODEL_WIDTH, KEY_VALUE_HEADS * HEAD_SIZE), jnp.float32) / math.sqrt(MODEL_WIDTH)
    return rotary_base.astype(jnp.bfloat16)


def plant(array, key, low, top_value):
    shape = array.shape
    index_at = [jax.random.randint(jax.random.fold_in(key, axis), (), 0, shape[axis]) for axis in range(len(shape))]
    array = array.at[tuple(index_at)].set(low)
    longest = shape.index(max(shape))
    index_at[longest] = (index_at[longest] + 1) % shape[longest]
    return array.at[tuple(index_at)].set(top_value)


def steps_of(stream_key, shape, cuts, smallest, largest):
    def one(position, blocks):
        steps = jax.random.uniform(jax.random.fold_in(jax.random.fold_in(stream_key, 6), position), (blocks,), jnp.float32, smallest / len(cuts), largest / len(cuts))
        return jnp.repeat(jnp.exp(steps), shape[position] // blocks).reshape((-1,) + (1,) * (len(shape) - position - 1))

    level = one(*cuts[0])
    for cut in cuts[1:]:
        level = level * one(*cut)
    return level


def gaussian(rng, dims, deviation, most, pieces=(), kind=jnp.bfloat16):
    factor_of = steps_of(rng, dims, pieces, -0.22, 0.18) if pieces else 1.0
    values = jax.random.normal(rng, dims, jnp.float32) * deviation * factor_of
    return jnp.minimum(jnp.maximum(values, -most), most).astype(kind)


def setup_inputs(seed: int = 0, part: int = 0) -> dict:
    key_of = jax.random.split(jax.random.key(seed), 8)
    part_splits = jax.random.split(jax.random.fold_in(key_of[7], part), 8)
    return {
        "layer_input": draw_layer_input(jax.random.fold_in(jax.random.fold_in(key_of[7], part), 71), part),
        "norm_gain": jnp.clip(1.0 + 0.15 * jax.random.normal(key_of[1], (MODEL_WIDTH,), jnp.float32), 0.25, 1.75),
        "query_weight": draw_query_weight(jax.random.fold_in(key_of[7], 71), part),
        "key_weight": draw_key_weight(jax.random.fold_in(key_of[7], 71), part),
        "value_matrix": gaussian(key_of[4], (MODEL_WIDTH, KEY_VALUE_HEADS * HEAD_SIZE), MODEL_WIDTH ** -0.5, 0.09375, ((1, 16),)),
        "output_weight": gaussian(key_of[5], (QUERY_HEADS * HEAD_SIZE, MODEL_WIDTH), (QUERY_HEADS * HEAD_SIZE) ** -0.5, 0.09375, ((0, 16),)),
        "keep_bits": plant((jax.random.randint(part_splits[6], (QUERY_HEADS, NB, NB), 0, 10) < 9).astype(jnp.int32), jax.random.fold_in(part_splits[6], 1), 0, 1),
    }


theta_base = 1000000.0

def apply_rotary(block, token_positions):
    half = block.shape[-1] // 2
    freqs = theta_base ** (-(jnp.arange(half, dtype=jnp.float32) * 2.0) / block.shape[-1])
    angles = token_positions[:, None] * freqs[None, :]
    cosine = jnp.cos(angles)
    sine = jnp.sin(angles)
    first = block[..., :half]
    second = block[..., half:]
    return jnp.concatenate([first * cosine - second * sine, second * cosine + first * sine], axis=-1)

def attend(query, key_rows, value_rows, keep_bits):
    heads, sequence_length, width = query.shape
    count = min(8, max(1, sequence_length // 512))
    height = sequence_length // count
    divisor = jnp.sqrt(jnp.float32(HEAD_SIZE))
    results = []
    for number in range(count):
        first_row = number * height
        last_row = first_row + height
        scores = jnp.einsum('hqd,hkd->hqk', query[:, first_row:last_row].astype(jnp.float32), key_rows[:, :last_row].astype(jnp.float32)) / divisor
        causal = jnp.arange(last_row)[None, :] <= jnp.arange(first_row, last_row)[:, None]
        scores = jnp.where(causal[None], scores, jnp.float32(-1e+30))
        highest = lax.optimization_barrier(jnp.max(scores, axis=-1, keepdims=True))
        expo_terms = jnp.exp(scores - highest)
        weights = expo_terms / lax.optimization_barrier(jnp.sum(expo_terms, axis=-1, keepdims=True))
        chosen_bits = keep_bits[:, first_row // BLOCK:last_row // BLOCK, :last_row // BLOCK].astype(jnp.float32)
        keeper = jnp.broadcast_to(chosen_bits[:, :, None, :, None], (heads, height // BLOCK, BLOCK, last_row // BLOCK, BLOCK)).reshape(heads, height, last_row)
        dropped = (weights * keeper / 0.9).astype(jnp.bfloat16)
        outcome = jnp.einsum('hqk,hkd->hqd', dropped.astype(jnp.float32), value_rows[:, :last_row].astype(jnp.float32))
        results.append(outcome.astype(jnp.bfloat16))
    return jnp.concatenate(results, axis=1)

def reference(layer_input, norm_gain, query_weight, key_weight, value_matrix, output_weight, keep_bits):
    sequence_length = layer_input.shape[0]
    inputs = layer_input.astype(jnp.float32)
    scaled = lax.rsqrt(lax.optimization_barrier(jnp.mean(inputs * inputs, axis=-1, keepdims=True)) + 1e-05)
    normed = (inputs * scaled * norm_gain[None, :]).astype(jnp.bfloat16)
    token_positions = jnp.arange(sequence_length).astype(jnp.float32)
    query_raw = jnp.dot(normed, query_weight, preferred_element_type=jnp.float32)
    key_unrotated = jnp.dot(normed, key_weight, preferred_element_type=jnp.float32).astype(jnp.bfloat16)
    value_rows = jnp.dot(normed, value_matrix, preferred_element_type=jnp.float32).astype(jnp.bfloat16)
    query = apply_rotary(query_raw.reshape(sequence_length, QUERY_HEADS, HEAD_SIZE).transpose(1, 0, 2), token_positions).astype(jnp.bfloat16)
    key_rows = apply_rotary(key_unrotated.astype(jnp.float32).reshape(sequence_length, KEY_VALUE_HEADS, HEAD_SIZE).transpose(1, 0, 2), token_positions).astype(jnp.bfloat16)
    value_rows = value_rows.reshape(sequence_length, KEY_VALUE_HEADS, HEAD_SIZE).transpose(1, 0, 2)
    query_group = QUERY_HEADS // KEY_VALUE_HEADS
    key_rows = jnp.repeat(key_rows, query_group, axis=0)
    value_rows = jnp.repeat(value_rows, query_group, axis=0)
    heads = attend(query, key_rows, value_rows, keep_bits)
    heads_out = heads.transpose(1, 0, 2).reshape(sequence_length, QUERY_HEADS * HEAD_SIZE)
    columns = QUERY_HEADS * HEAD_SIZE // N_TENSOR
    grouped = heads_out.reshape(sequence_length, N_TENSOR, columns).transpose(1, 0, 2)
    weight_rows = output_weight.reshape(N_TENSOR, columns, MODEL_WIDTH)

    def add_part(total, items):
        part_in, part_rows = items
        part = lax.optimization_barrier(jnp.dot(part_in, part_rows, preferred_element_type=jnp.float32).astype(jnp.bfloat16))
        return (total + part.astype(jnp.float32), None)
    total, unused = lax.scan(add_part, jnp.zeros((sequence_length, MODEL_WIDTH), jnp.float32), (grouped, weight_rows))
    return (inputs + total).astype(jnp.bfloat16)
```

```python
import functools
import math

import jax
import jax.numpy as jnp
from jax import lax
from jax.experimental import pallas as pl
from jax.experimental.pallas import tpu as pltpu
from jax.sharding import Mesh
from jax.sharding import PartitionSpec as P

HEAD = 128
BLOCK = 64
WIDTH = 4096
Z = 8
HALF = 32
COLS = 2048
THETA = 1000000.0
RIGHT = [(i, (i + 1) % Z) for i in range(Z)]
LEFT = [(i, (i - 1) % Z) for i in range(Z)]
NEAR = [0, -1, 1, -2, 2, -3, 3]
BF = jnp.bfloat16
F32 = jnp.float32
DEPTH = 1024


def proj_kernel(places, rows, *refs):
    n = len(places)
    pieces = refs[:n]
    gain, wq, wp, wkv, cos, sin, q, k, v, xs, acc, ss = refs[n:]
    step = pl.program_id(0)
    last = pl.num_programs(0) - 1

    @pl.when(step == 0)
    def _():
        acc[...] = jnp.zeros_like(acc)
        ss[...] = jnp.zeros_like(ss)

    g = gain[...]
    for ref, (start, count) in zip(pieces, places):
        x = ref[...].astype(F32)
        sq = x * x
        part = sq[:, :HEAD]
        for i in range(1, DEPTH // HEAD):
            part = part + sq[:, i * HEAD : (i + 1) * HEAD]
        ss[start : start + count, :] += part
        xs[start : start + count, :] = (x * g).astype(BF)
    x = xs[...]
    acc[:, 0:256] += jnp.dot(x, wq[...], preferred_element_type=F32)
    acc[:, 256:512] += jnp.dot(x, wp[...], preferred_element_type=F32)
    acc[:, 512:768] += jnp.dot(x, wkv[...], preferred_element_type=F32)

    @pl.when(step == last)
    def _():
        scale = lax.rsqrt(jnp.sum(ss[...], axis=-1, keepdims=True) / WIDTH + 1e-05)
        c = cos[...]
        s = sin[...]

        def rot(t):
            return t * c + pltpu.roll(t, HEAD // 2, 1) * s

        factor = math.log2(math.e) / math.sqrt(HEAD)
        for h in range(4):
            t = acc[:, h * HEAD : (h + 1) * HEAD] * scale
            t = (rot(t) * factor).astype(BF)
            q[:, h, :, :] = t.reshape(rows // BLOCK, BLOCK, HEAD)
        t = (acc[:, 512:640] * scale).astype(BF).astype(F32)
        k[...] = rot(t).astype(BF)
        v[...] = (acc[:, 640:768] * scale).astype(BF)


def project(pieces, places, gain, wq, wp, wkv, cos, sin):
    rows = sum(count for _, count in places)
    whole = lambda i: (0, 0)
    wide = lambda i: (i, 0)
    return pl.pallas_call(
        functools.partial(proj_kernel, places, rows),
        grid=(WIDTH // DEPTH,),
        in_specs=[pl.BlockSpec((count, DEPTH), lambda i: (0, i)) for _, count in places]
        + [pl.BlockSpec((1, DEPTH), lambda i: (0, i))]
        + [pl.BlockSpec((DEPTH, 256), wide)] * 3
        + [pl.BlockSpec((rows, HEAD), whole)] * 2,
        out_specs=[
            pl.BlockSpec((rows // BLOCK, 4, BLOCK, HEAD), lambda i: (0, 0, 0, 0)),
            pl.BlockSpec((rows, HEAD), whole),
            pl.BlockSpec((rows, HEAD), whole),
        ],
        out_shape=[
            jax.ShapeDtypeStruct((rows // BLOCK, 4, BLOCK, HEAD), BF),
            jax.ShapeDtypeStruct((rows, HEAD), BF),
            jax.ShapeDtypeStruct((rows, HEAD), BF),
        ],
        scratch_shapes=[
            pltpu.VMEM((rows, DEPTH), BF),
            pltpu.VMEM((rows, 768), F32),
            pltpu.VMEM((rows, HEAD), F32),
        ],
        compiler_params=pltpu.CompilerParams(vmem_limit_bytes=32 << 20),
        cost_estimate=pl.CostEstimate(
            flops=2 * rows * WIDTH * 768,
            bytes_accessed=2 * WIDTH * (rows + 768),
            transcendentals=0,
        ),
        name="project",
    )(*pieces, gain, wq, wp, wkv, cos, sin)


def attend_kernel(far, base, q, keep, key, value, kpos, wo, wp, *refs):
    outs, heads = refs[:-1], refs[-1]
    j = pl.program_id(0)
    qpos = base[j] + lax.broadcasted_iota(jnp.int32, (BLOCK, 1), 0)
    mask = kpos[...] <= qpos
    kk = key[...]
    vv = value[...]
    for h in range(4):
        s = lax.dot_general(
            q[0, h], kk, (((1,), (1,)), ((), ())), preferred_element_type=F32
        )
        s = jnp.where(mask, s, -1e30)
        e = jnp.exp2(s - jnp.max(s, axis=-1, keepdims=True))
        total = jnp.sum(e, axis=-1, keepdims=True)
        p = (e * keep[0, h][None, :]).astype(BF)
        o = jnp.dot(p, vv, preferred_element_type=F32)
        heads[:, h * HEAD : (h + 1) * HEAD] = (o / (total * 0.9)).astype(BF)
    left = heads[:, :256]
    right = heads[:, 256:]
    for c in range(2):
        cols = slice(c * COLS, (c + 1) * COLS)
        t = jnp.dot(left, wo[:, cols], preferred_element_type=F32)
        t = (t + jnp.dot(right, wp[:, cols], preferred_element_type=F32)).astype(BF)
        if far:
            outs[c][...] = t[:HALF]
            outs[2 + c][...] = t[HALF:]
        else:
            outs[c][0] = t


def attend(far, base, q, keep, key, value, kpos, wo, wp):
    n = q.shape[0]
    whole = lambda j, b: (0, 0)
    if far:
        out_specs = [pl.BlockSpec((HALF, COLS), whole)] * 4
        out_shape = [jax.ShapeDtypeStruct((HALF, COLS), BF)] * 4
    else:
        out_specs = [pl.BlockSpec((1, BLOCK, COLS), lambda j, b: (j, 0, 0))] * 2
        out_shape = [jax.ShapeDtypeStruct((n, BLOCK, COLS), BF)] * 2
    return pl.pallas_call(
        functools.partial(attend_kernel, far),
        grid_spec=pltpu.PrefetchScalarGridSpec(
            num_scalar_prefetch=1,
            grid=(n,),
            in_specs=[
                pl.BlockSpec((1, 4, BLOCK, HEAD), lambda j, b: (j, 0, 0, 0)),
                pl.BlockSpec((1, 4, 1024), lambda j, b: (j, 0, 0)),
                pl.BlockSpec((1024, HEAD), whole),
                pl.BlockSpec((1024, HEAD), whole),
                pl.BlockSpec((1, 1024), whole),
                pl.BlockSpec((256, WIDTH), whole),
                pl.BlockSpec((256, WIDTH), whole),
            ],
            out_specs=out_specs,
            scratch_shapes=[pltpu.VMEM((BLOCK, 512), BF)],
        ),
        out_shape=out_shape,
        compiler_params=pltpu.CompilerParams(vmem_limit_bytes=32 << 20),
        cost_estimate=pl.CostEstimate(
            flops=n * (2 * 2 * 256 * 1024 * 128 + 2 * 64 * 512 * 4096),
            bytes_accessed=(4 << 20) + n * 600000,
            transcendentals=n * 256 * 1024,
        ),
        name="attend",
    )(base, q, keep, key, value, kpos, wo, wp)


def swap_weights(array, core):
    got = lax.ppermute(array, ("xl", "xh"), [(i, 3 - i) for i in range(4)])
    other = lax.ppermute(got, "c", [(0, 1), (1, 0)])
    return jnp.where(
        core == 0,
        jnp.concatenate([got, other], axis=0),
        jnp.concatenate([other, got], axis=0),
    )


def pair(array):
    return lax.ppermute(array, "xh", [(0, 1), (1, 0)])


def add(a, b):
    return (a.astype(F32) + b.astype(F32)).astype(BF)


def on_device(
    layer_input, norm_gain, query_weight, key_weight, value_matrix, output_weight, keep_bits
):
    core = lax.axis_index("c")
    z = lax.axis_index("z")
    xh = lax.axis_index("xh")

    chunks = [layer_input[:HALF], layer_input[HALF:]]
    pieces = [layer_input]
    places = [(0, BLOCK)]
    r = list(chunks)
    l = list(chunks)
    for s in range(3):
        for c in range(2):
            r[c] = lax.ppermute(r[c], "z", RIGHT)
            l[c] = lax.ppermute(l[c], "z", LEFT)
        pieces += r + l
        at = BLOCK * (1 + 2 * s)
        places += [(at + i * HALF, HALF) for i in range(4)]
    last = [lax.ppermute(r[0], "z", RIGHT), lax.ppermute(l[1], "z", LEFT)]
    last_places = [(0, HALF), (HALF, HALF)]

    rows = WIDTH // 2
    mine = jnp.concatenate(
        [
            lax.dynamic_slice_in_dim(w, core * rows, rows, 0)
            for w in (query_weight, key_weight, value_matrix)
        ],
        axis=1,
    )
    theirs = swap_weights(mine, core)
    wp = theirs[:, :256]
    k_other = theirs[:, 256:320]
    v_other = theirs[:, 320:384]
    first = xh == 0
    wkv = jnp.where(
        first,
        jnp.concatenate([key_weight, k_other, value_matrix, v_other], axis=1),
        jnp.concatenate([k_other, key_weight, v_other, value_matrix], axis=1),
    )
    wo_other = swap_weights(lax.dynamic_slice_in_dim(output_weight, core * 128, 128, 0), core)

    order = (z + jnp.array(NEAR + [4], jnp.int32)) % Z
    starts = (order * 2 + xh) * BLOCK
    starts_other = (order * 2 + (1 - xh)) * BLOCK
    inner = jnp.arange(BLOCK, dtype=jnp.int32)
    kpos = jnp.concatenate(
        [(starts[:, None] + inner).reshape(-1), (starts_other[:, None] + inner).reshape(-1)]
    )
    token_positions = kpos[:512].astype(F32)
    freqs = THETA ** (-(jnp.arange(HEAD // 2, dtype=F32) * 2.0) / HEAD)
    angles = token_positions[:, None] * freqs[None, :]
    cosine = jnp.cos(angles)
    sine = jnp.sin(angles)
    cosine = jnp.concatenate([cosine, cosine], axis=1)
    sine = jnp.concatenate([-sine, sine], axis=1)

    bits = jnp.concatenate([keep_bits, pair(keep_bits)], axis=0).astype(F32)
    blocks = jnp.arange(16, dtype=jnp.int32)
    q_hot = (starts[:, None] // BLOCK == blocks[None, :]).astype(F32)
    k_blocks = jnp.concatenate([starts, starts_other]) // BLOCK
    k_hot = (k_blocks[:, None] == blocks[None, :]).astype(F32)
    keep = jnp.einsum("jq,hqk,mk->jhm", q_hot, bits, k_hot)
    keep = jnp.repeat(keep, BLOCK, axis=2)

    gain = norm_gain[None, :]
    q_near, k_near, v_near = project(
        pieces, places, gain, query_weight, wp, wkv, cosine[:448], sine[:448]
    )
    kv_near = pair(jnp.stack([k_near, v_near]))
    q_far, k_far, v_far = project(
        last, last_places, gain, query_weight, wp, wkv, cosine[448:], sine[448:]
    )
    kv_far = pair(jnp.stack([k_far, v_far]))
    key = jnp.concatenate([k_near, k_far, kv_near[0], kv_far[0]], axis=0)
    value = jnp.concatenate([v_near, v_far, kv_near[1], kv_far[1]], axis=0)
    kpos = kpos[None, :]

    far = attend(
        True, starts[7:], q_far, keep[7:], key, value, kpos, output_weight, wo_other
    )
    near = attend(
        False, starts[:7], q_near, keep[:7], key, value, kpos, output_weight, wo_other
    )
    total = []
    for c in range(2):
        block = lambda d: near[c][NEAR.index(d)]
        r = lax.ppermute(far[c], "z", RIGHT)
        l = lax.ppermute(far[2 + c], "z", LEFT)
        r = jnp.concatenate([add(r, block(3)[:HALF]), block(3)[HALF:]])
        l = jnp.concatenate([block(-3)[:HALF], add(l, block(-3)[HALF:])])
        for d in (2, 1):
            r = add(lax.ppermute(r, "z", RIGHT), block(d))
            l = add(lax.ppermute(l, "z", LEFT), block(-d))
        r = lax.ppermute(r, "z", RIGHT)
        l = lax.ppermute(l, "z", LEFT)
        total.append(block(0).astype(F32) + r.astype(F32) + l.astype(F32))
    total = jnp.concatenate(total, axis=1)
    return (layer_input.astype(F32) + total).astype(BF)


def solution(mesh):
    split = Mesh(mesh.devices.reshape(2, 4, 2, Z, 2), ("xl", "y", "c", "z", "xh"))
    every = ("xl", "y", "c", "z", "xh")
    tensor = ("z", "xh")
    return jax.shard_map(
        on_device,
        mesh=split,
        in_specs=(
            P(every, None),
            P(),
            P(None, tensor),
            P(None, tensor),
            P(None, tensor),
            P(tensor, None),
            P(every, None, None),
        ),
        out_specs=P(every, None),
        check_vma=False,
    )
```

```python
import functools
import math

import jax
import jax.numpy as jnp
import numpy as np
from jax import lax
from jax.experimental import pallas as pl
from jax.experimental.pallas import tpu as pltpu
from jax.sharding import Mesh
from jax.sharding import PartitionSpec as P

HEAD = 128
BLOCK = 64
WIDTH = 4096
Z = 8
HALF = 32
COLS = 2048
THETA = 1000000.0
RIGHT = [(i, (i + 1) % Z) for i in range(Z)]
LEFT = [(i, (i - 1) % Z) for i in range(Z)]
NEAR = [0, -1, 1, -2, 2, -3, 3]
BF = jnp.bfloat16
F32 = jnp.float32
TINY = pl.CostEstimate(flops=1000, bytes_accessed=1000, transcendentals=0)


def slot_block(slot, z):
    offset = jnp.where(slot % 2 == 1, -((slot + 1) // 2), slot // 2)
    return lax.rem(z + offset + Z, Z)


def tables():
    freqs = THETA ** (-np.arange(HEAD // 2) * 2.0 / HEAD)

    def table(positions):
        angles = positions[:, None] * freqs[None, :]
        cosine, sine = np.cos(angles), np.sin(angles)
        return np.stack(
            [np.concatenate([cosine, cosine], 1), np.concatenate([-sine, sine], 1)]
        ).astype(np.float32)

    return table(np.arange(16) * float(BLOCK))[:, :, None, :], table(np.arange(BLOCK) * 1.0)


def load_tokens(places, pieces, gain, xs, ss, step):
    depth = xs.shape[1]
    g = gain[...]
    for ref, (start, count) in zip(pieces, places):
        x = ref[...].astype(F32)
        sq = x * x
        part = sq[:, :HEAD]
        for i in range(1, depth // HEAD):
            part = part + sq[:, i * HEAD : (i + 1) * HEAD]
        at = slice(start, start + count)
        ss[at] = jnp.where(step == 0, part, ss[at] + part)
        xs[at] = (x * g).astype(BF)


def angles_of(outer, inner, slot, meta):
    block = slot_block(jnp.int32(slot), meta[1]) * 2 + meta[2]
    co = outer[0, block]
    so = outer[1, block]
    return inner[0] * co - inner[1] * so, inner[1] * co + inner[0] * so


def gather_sum(acc, term, step):
    acc[...] = jnp.where(step == 0, term, acc[...] + term)


def kv_kernel(places, slots, waits, meta, *refs):
    n = len(places)
    pieces = refs[:n]
    gain, kt, vt, got, other, outer, inner = refs[n : n + 7]
    kv, xs, kvs, acc, ss = refs[n + 7 + waits :]
    step = pl.program_id(0)
    early = step < pl.num_programs(0) // 2
    load_tokens(places, pieces, gain, xs, ss, step)
    kvs[0:64] = kt[...]
    kvs[128:192] = vt[...]
    for i in range(xs.shape[1] // 256):
        at = slice(i * 256, (i + 1) * 256)
        low = slice(i * 128, i * 128 + 64)
        high = slice(i * 128 + 64, i * 128 + 128)
        kvs[64:128, at] = jnp.where(early, got[low], other[low])
        kvs[192:256, at] = jnp.where(early, got[high], other[high])
    term = lax.dot_general(
        xs[...], kvs[...], (((1,), (1,)), ((), ())), preferred_element_type=F32
    )
    gather_sum(acc, term, step)

    @pl.when(step == pl.num_programs(0) - 1)
    def _():
        first = meta[2] == 0

        def ordered(t):
            return jnp.where(first, t, pltpu.roll(t, HEAD // 2, 1))

        scale = lax.rsqrt(jnp.sum(ss[...], axis=-1, keepdims=True) / WIDTH + 1e-05)
        kv[1] = ordered(acc[:, HEAD:] * scale).astype(BF)
        key = ordered(acc[:, :HEAD] * scale).astype(BF).astype(F32)
        turned = pltpu.roll(key, HEAD // 2, 1)
        for i, slot in enumerate(slots):
            at = slice(i * BLOCK, (i + 1) * BLOCK)
            c, s = angles_of(outer, inner, slot, meta)
            kv[0, at] = (key[at] * c + turned[at] * s).astype(BF)


def q_kernel(places, slots, waits, meta, *refs):
    n = len(places)
    pieces = refs[:n]
    gain, wq, got, other, outer, inner = refs[n : n + 6]
    q, xs, acc, ss = refs[n + 6 + waits :]
    step = pl.program_id(0)
    load_tokens(places, pieces, gain, xs, ss, step)
    x = xs[...]
    gather_sum(acc.at[:, 0:256], jnp.dot(x, wq[...], preferred_element_type=F32), step)
    w = jnp.where(step < pl.num_programs(0) // 2, got[...], other[...])
    gather_sum(acc.at[:, 256:512], jnp.dot(x, w, preferred_element_type=F32), step)

    @pl.when(step == pl.num_programs(0) - 1)
    def _():
        core = meta[0]
        factor = math.log2(math.e) / math.sqrt(HEAD)
        scale = factor * lax.rsqrt(jnp.sum(ss[...], axis=-1, keepdims=True) / WIDTH + 1e-05)
        for i, slot in enumerate(slots):
            at = slice(i * BLOCK, (i + 1) * BLOCK)
            c, s = angles_of(outer, inner, slot, meta)
            c = c * scale[at]
            s = s * scale[at]
            heads = []
            for h in range(4):
                t = acc[at, h * HEAD : (h + 1) * HEAD]
                heads.append((t * c + pltpu.roll(t, HEAD // 2, 1) * s).astype(BF))
            q[i, 0] = heads[0]
            q[i, 1] = heads[1]
            q[i, 2] = jnp.where(core == 0, heads[2], heads[3])
            q[i, 3] = jnp.where(core == 0, heads[3], heads[2])


def project(queries, after, meta, pieces, places, slots, gain, own, got, other):
    n = len(slots)
    rows = n * BLOCK
    depth = 1024 if queries else 2048
    steps = WIDTH // depth
    outer, inner = tables()
    turn = lambda i, m: lax.rem(steps // 2 * m[0] + i, steps)
    across = lambda i, m: (0, turn(i, m))
    soon = lambda i: jnp.minimum(i, steps // 2 - 1)
    late = lambda i: jnp.maximum(i - steps // 2, 0)
    zero = lambda k: lambda i, m: (0,) * k
    if queries:
        weights = [
            pl.BlockSpec((depth, 256), lambda i, m: (turn(i, m), 0)),
            pl.BlockSpec((depth, 256), lambda i, m: (soon(i), 0)),
            pl.BlockSpec((depth, 256), lambda i, m: (late(i), 0)),
        ]
        shape = (n, 4, BLOCK, HEAD)
        scratch = [pltpu.VMEM((rows, depth), BF), pltpu.VMEM((rows, 512), F32)]
    else:
        weights = [
            pl.BlockSpec((64, depth), across),
            pl.BlockSpec((64, depth), across),
            pl.BlockSpec((depth // 2, 256), lambda i, m: (steps + soon(i), 0)),
            pl.BlockSpec((depth // 2, 256), lambda i, m: (steps + late(i), 0)),
        ]
        shape = (2, rows, HEAD)
        scratch = [
            pltpu.VMEM((rows, depth), BF),
            pltpu.VMEM((256, depth), BF),
            pltpu.VMEM((rows, 256), F32),
        ]
    return pl.pallas_call(
        functools.partial(q_kernel if queries else kv_kernel, places, slots, len(after)),
        grid_spec=pltpu.PrefetchScalarGridSpec(
            num_scalar_prefetch=1,
            grid=(steps,),
            in_specs=[pl.BlockSpec((count, depth), across) for _, count in places]
            + [pl.BlockSpec((1, depth), across)]
            + weights
            + [pl.BlockSpec((2, 16, 1, HEAD), zero(4)), pl.BlockSpec((2, BLOCK, HEAD), zero(3))]
            + [pl.BlockSpec(memory_space=pl.ANY)] * len(after),
            out_specs=pl.BlockSpec(shape, zero(len(shape))),
            scratch_shapes=scratch + [pltpu.VMEM((rows, HEAD), F32)],
        ),
        out_shape=jax.ShapeDtypeStruct(shape, BF),
        compiler_params=pltpu.CompilerParams(vmem_limit_bytes=56 << 20),
        cost_estimate=TINY,
        name="queries" if queries else "keys",
    )(meta, *pieces, gain, *own, got, other, outer, inner, *after)


def attend_kernel(slots, waits, meta, q, bits, kv_near, kv_far, their_near, their_far, *refs):
    wo, wp_got, wp_other = refs[:3]
    outs = refs[3 + waits : -3]
    heads, key, value = refs[-3:]
    nb = len(slots)
    for i, target in ((0, key), (1, value)):
        target[0:448] = kv_near[i]
        target[448:512] = kv_far[i]
        target[512:960] = their_near[i * 448 : (i + 1) * 448]
        target[960:1024] = their_far[i]
    z = meta[1]
    xh = meta[2]
    column = lax.broadcasted_iota(jnp.int32, (1, 1024), 1)
    mine = column < 512
    kblock = slot_block((column // BLOCK) % 8, z) * 2 + jnp.where(mine, xh, 1 - xh)
    kpos = kblock * BLOCK + column % BLOCK
    lane = lax.broadcasted_iota(jnp.int32, (HEAD, 1024), 0)
    hot = [(lane == kblock + h * 16).astype(BF) for h in range(2)]
    core = meta[0]
    for b in range(nb):
        block = slot_block(jnp.int32(slots[b]), z) * 2 + xh
        qpos = block * BLOCK + lax.broadcasted_iota(jnp.int32, (BLOCK, 1), 0)
        row = (lax.broadcasted_iota(jnp.int32, (8, 16), 1) == block).astype(BF)
        ours = jnp.dot(row, bits[...], preferred_element_type=F32).astype(BF)
        theirs = jnp.dot(row, their_near[896:912], preferred_element_type=F32).astype(BF)
        keep = [jnp.dot(ours, hot[h], preferred_element_type=F32)[0:1] for h in range(2)]
        pair = [jnp.dot(theirs, hot[h], preferred_element_type=F32)[0:1] for h in range(2)]
        keep.append(jnp.where(core == 0, pair[0], pair[1]))
        keep.append(jnp.where(core == 0, pair[1], pair[0]))
        bias = jnp.where(kpos <= qpos, 0.0, -1e30)
        s = lax.dot_general(
            q[slots[b]].reshape(256, HEAD),
            key[...],
            (((1,), (1,)), ((), ())),
            preferred_element_type=F32,
        )
        s = s.reshape(4, BLOCK, 1024) + bias[None]
        e = jnp.exp2(s - jnp.max(s, axis=-1, keepdims=True))
        total = jnp.sum(e, axis=-1, keepdims=True)
        p = jnp.concatenate([(e[h] * keep[h]).astype(BF) for h in range(4)], axis=0)
        o = jnp.dot(p, value[...], preferred_element_type=F32).reshape(4, BLOCK, HEAD)
        o = (o / (total * 0.9)).astype(BF)
        for h in range(4):
            heads[b * BLOCK : (b + 1) * BLOCK, h * HEAD : (h + 1) * HEAD] = o[h]
    x = heads[...]
    piece = 512
    for c in range(WIDTH // piece):
        cols = slice(c * piece, (c + 1) * piece)
        w = jnp.concatenate([wo[:, cols], wp_got[:, cols], wp_other[:, cols]], axis=0)
        t = jnp.dot(x, w, preferred_element_type=F32).astype(BF)
        half = c // (COLS // piece)
        at = slice(c * piece - half * COLS, (c + 1) * piece - half * COLS)
        for b in range(nb):
            outs[half * nb + b][:, at] = t[b * BLOCK : (b + 1) * BLOCK]


def attend(slots, after, meta, q, *rest):
    nb = len(slots)
    out_shape = [jax.ShapeDtypeStruct((BLOCK, COLS), BF)] * (2 * nb)
    vmem = pl.BlockSpec(memory_space=pltpu.VMEM)
    return pl.pallas_call(
        functools.partial(attend_kernel, slots, len(after)),
        in_specs=[pl.BlockSpec(memory_space=pltpu.SMEM), vmem]
        + [vmem] * 8
        + [pl.BlockSpec(memory_space=pl.ANY)] * len(after),
        out_specs=[vmem] * len(out_shape),
        out_shape=out_shape,
        scratch_shapes=[
            pltpu.VMEM((nb * BLOCK, 512), BF),
            pltpu.VMEM((1024, HEAD), BF),
            pltpu.VMEM((1024, HEAD), BF),
        ],
        compiler_params=pltpu.CompilerParams(vmem_limit_bytes=32 << 20),
        cost_estimate=TINY,
        name="attend",
    )(meta, q, *rest, *after)


def pick_kernel(meta, wq, kt, vt, out):
    half = WIDTH // 2
    out[0:half] = wq[...]
    for i in range(half // 256):
        at = slice(i * 256, (i + 1) * 256)
        row = half + i * 128
        out[row : row + 64] = kt[:, at]
        out[row + 64 : row + 128] = vt[:, at]


def pick(meta, wq, kt, vt):
    half = WIDTH // 2
    return pl.pallas_call(
        pick_kernel,
        grid_spec=pltpu.PrefetchScalarGridSpec(
            num_scalar_prefetch=1,
            grid=(1,),
            in_specs=[
                pl.BlockSpec((half, 256), lambda i, m: (m[0], 0)),
                pl.BlockSpec((64, half), lambda i, m: (0, m[0])),
                pl.BlockSpec((64, half), lambda i, m: (0, m[0])),
            ],
            out_specs=pl.BlockSpec((half + half // 2, 256), lambda i, m: (0, 0)),
        ),
        out_shape=jax.ShapeDtypeStruct((half + half // 2, 256), BF),
        compiler_params=pltpu.CompilerParams(vmem_limit_bytes=56 << 20),
        cost_estimate=TINY,
        name="pick",
    )(meta, wq, kt, vt)


def gate_kernel(*refs):
    pass


def gate(arrays, after):
    n = len(arrays)
    anywhere = pl.BlockSpec(memory_space=pl.ANY)
    return pl.pallas_call(
        gate_kernel,
        in_specs=[anywhere] * (n + len(after)),
        out_specs=[anywhere] * n,
        out_shape=[jax.ShapeDtypeStruct(a.shape, a.dtype) for a in arrays],
        input_output_aliases={i: i for i in range(n)},
        cost_estimate=TINY,
        name="gate",
    )(*arrays, *after)


def from_x(array):
    return lax.ppermute(array, ("xl", "xh"), [(i, 3 - i) for i in range(4)])


def from_core(array):
    return lax.ppermute(array, "c", [(0, 1), (1, 0)])


def pair(array):
    return lax.ppermute(array, "xh", [(0, 1), (1, 0)])


def add(a, b):
    return (a.astype(F32) + b.astype(F32)).astype(BF)


def on_device(
    layer_input, norm_gain, query_weight, key_weight, value_matrix, output_weight, keep_bits
):
    core = lax.axis_index("c")
    z = lax.axis_index("z")
    xh = lax.axis_index("xh")

    pieces = [layer_input]
    places = [(0, BLOCK)]
    r = layer_input
    l = layer_input
    for s in range(3):
        r = lax.ppermute(r, "z", RIGHT)
        l = lax.ppermute(l, "z", LEFT)
        pieces += [r, l]
        at = BLOCK * (1 + 2 * s)
        places += [(at, BLOCK), (at + BLOCK, BLOCK)]
        if s == 1:
            step_two = [r, l]
    step_three = [r, l]
    last = [lax.ppermute(r[:HALF], "z", RIGHT), lax.ppermute(l[HALF:], "z", LEFT)]
    last_places = [(0, HALF), (HALF, HALF)]

    meta = jnp.stack([core, z, xh]).astype(jnp.int32)
    kt = key_weight.T
    vt = value_matrix.T
    got = from_x(pick(meta, query_weight, kt, vt))
    (got,) = gate([got], step_three)
    other = from_core(got)
    wo_mine = lax.dynamic_slice_in_dim(output_weight, core * HEAD, HEAD, 0)
    (wo_mine,) = gate([wo_mine], [step_two[0]])
    wo_got = from_x(wo_mine)

    bits = keep_bits.astype(BF).transpose(1, 0, 2).reshape(16, 32)
    bits = jnp.pad(bits, ((0, 0), (0, HEAD - 32)))

    gain = norm_gain[None, :]
    kv_near = project(False, [], meta, pieces, places, range(7), gain, (kt, vt), got, other)
    their_near = pair(jnp.concatenate([kv_near.reshape(896, HEAD), bits]))
    kv_far = project(False, [kv_near], meta, last, last_places, [7], gain, (kt, vt), got, other)
    their_far = pair(kv_far)
    everything = places + [(448 + start, count) for start, count in last_places]
    q = project(
        True, [kv_far], meta, pieces + last, everything, range(8), gain, (query_weight,), got, other
    )
    (wo_got,) = gate([wo_got], [q])
    wo_other = from_core(wo_got)
    shared = (bits, kv_near, kv_far, their_near, their_far, output_weight, wo_got, wo_other)

    near = {}

    def compute(slots, after):
        got = attend(slots, after, meta, q, *shared)
        for i, slot in enumerate(slots):
            near[(NEAR + [4])[slot]] = (got[i], got[len(slots) + i])
        return got

    block = lambda d, c: near[d][c]
    done = compute([7, 5, 6], [])
    compute([3, 4, 0, 1, 2], [done[0]])
    far = near[4]
    r = [lax.ppermute(far[0], "z", RIGHT), None]
    l = [None, lax.ppermute(far[1], "z", LEFT)]
    r = [add(r[0], block(3, 0)), block(3, 1)]
    l = [block(-3, 0), add(l[1], block(-3, 1))]
    for d in (2, 1):
        for c in range(2):
            r[c] = add(lax.ppermute(r[c], "z", RIGHT), block(d, c))
            l[c] = add(lax.ppermute(l[c], "z", LEFT), block(-d, c))
    total = []
    for c in range(2):
        right = lax.ppermute(r[c], "z", RIGHT)
        left = lax.ppermute(l[c], "z", LEFT)
        total.append(block(0, c).astype(F32) + right.astype(F32) + left.astype(F32))
    total = jnp.concatenate(total, axis=1)
    return (layer_input.astype(F32) + total).astype(BF)


def solution(mesh):
    split = Mesh(mesh.devices.reshape(2, 4, 2, Z, 2), ("xl", "y", "c", "z", "xh"))
    every = ("xl", "y", "c", "z", "xh")
    tensor = ("z", "xh")
    return jax.shard_map(
        on_device,
        mesh=split,
        in_specs=(
            P(every, None),
            P(),
            P(None, tensor),
            P(None, tensor),
            P(None, tensor),
            P(tensor, None),
            P(every, None, None),
        ),
        out_specs=P(every, None),
        check_vma=False,
    )
```

```python
import functools
import math

import jax
import jax.numpy as jnp
import numpy as np
from jax import lax
from jax.experimental import pallas as pl
from jax.experimental.pallas import tpu as pltpu
from jax.sharding import Mesh
from jax.sharding import PartitionSpec as P

HEAD = 128
BLOCK = 64
WIDTH = 4096
Z = 8
HALF = 32
COLS = 2048
THETA = 1000000.0
RIGHT = [(i, (i + 1) % Z) for i in range(Z)]
LEFT = [(i, (i - 1) % Z) for i in range(Z)]
NEAR = [0, -1, 1, -2, 2, -3, 3]
BF = jnp.bfloat16
F32 = jnp.float32
TINY = pl.CostEstimate(flops=1000, bytes_accessed=1000, transcendentals=0)


def slot_block(slot, z):
    offset = jnp.where(slot % 2 == 1, -((slot + 1) // 2), slot // 2)
    return lax.rem(z + offset + Z, Z)


def tables():
    freqs = THETA ** (-np.arange(HEAD // 2) * 2.0 / HEAD)

    def table(positions):
        angles = positions[:, None] * freqs[None, :]
        cosine, sine = np.cos(angles), np.sin(angles)
        return np.stack(
            [np.concatenate([cosine, cosine], 1), np.concatenate([-sine, sine], 1)]
        ).astype(np.float32)

    return table(np.arange(16) * float(BLOCK))[:, :, None, :], table(np.arange(BLOCK) * 1.0)


def load_tokens(places, pieces, gain, xs, ss, step):
    depth = xs.shape[1]
    g = gain[...]
    for ref, (start, count) in zip(pieces, places):
        x = ref[...].astype(F32)
        sq = x * x
        part = sq[:, :HEAD]
        for i in range(1, depth // HEAD):
            part = part + sq[:, i * HEAD : (i + 1) * HEAD]
        at = slice(start, start + count)
        ss[at] = jnp.where(step == 0, part, ss[at] + part)
        xs[at] = (x * g).astype(BF)


def angles_of(outer, inner, slot, meta):
    block = slot_block(jnp.int32(slot), meta[1]) * 2 + meta[2]
    co = outer[0, block]
    so = outer[1, block]
    return inner[0] * co - inner[1] * so, inner[1] * co + inner[0] * so


def gather_sum(acc, term, step):
    acc[...] = jnp.where(step == 0, term, acc[...] + term)


def kv_kernel(places, slots, waits, meta, *refs):
    n = len(places)
    pieces = refs[:n]
    gain, kt, vt = refs[n : n + 3]
    theirs = refs[n + 3 : n + 7]
    outer, inner = refs[n + 7 : n + 9]
    kv, xs, kvs, acc, ss = refs[n + 9 + waits :]
    step = pl.program_id(0)
    load_tokens(places, pieces, gain, xs, ss, step)
    kvs[0:64] = kt[...]
    kvs[128:192] = vt[...]
    quarter = WIDTH // 4
    for turn in range(2):

        @pl.when(step == turn)
        def _():
            for t, base in ((0, meta[3] * quarter), (1, (1 - meta[3]) * quarter)):
                part = theirs[2 * turn + t]
                for i in range(quarter // 256):
                    at = pl.ds(pl.multiple_of(base + i * 256, 256), 256)
                    kvs[64:128, at] = part[i * 128 : i * 128 + 64]
                    kvs[192:256, at] = part[i * 128 + 64 : i * 128 + 128]

    term = lax.dot_general(
        xs[...], kvs[...], (((1,), (1,)), ((), ())), preferred_element_type=F32
    )
    gather_sum(acc, term, step)

    @pl.when(step == pl.num_programs(0) - 1)
    def _():
        first = meta[2] == 0

        def ordered(t):
            return jnp.where(first, t, pltpu.roll(t, HEAD // 2, 1))

        scale = lax.rsqrt(jnp.sum(ss[...], axis=-1, keepdims=True) / WIDTH + 1e-05)
        kv[1] = ordered(acc[:, HEAD:] * scale).astype(BF)
        key = ordered(acc[:, :HEAD] * scale).astype(BF).astype(F32)
        turned = pltpu.roll(key, HEAD // 2, 1)
        for i, slot in enumerate(slots):
            at = slice(i * BLOCK, (i + 1) * BLOCK)
            c, s = angles_of(outer, inner, slot, meta)
            kv[0, at] = (key[at] * c + turned[at] * s).astype(BF)


def q_kernel(places, slots, waits, meta, *refs):
    n = len(places)
    pieces = refs[:n]
    gain, wq = refs[n : n + 2]
    theirs = refs[n + 2 : n + 6]
    outer, inner = refs[n + 6 : n + 8]
    q, xs, acc, ss = refs[n + 8 + waits :]
    step = pl.program_id(0)
    load_tokens(places, pieces, gain, xs, ss, step)
    x = xs[...]
    gather_sum(acc.at[:, 0:256], jnp.dot(x, wq[...], preferred_element_type=F32), step)
    for turn in range(4):

        @pl.when(step == turn // 2)
        def _():
            place = meta[3] if turn % 2 == 0 else 1 - meta[3]
            quarter = WIDTH // 4
            columns = pl.ds(pl.multiple_of(place * quarter, quarter), quarter)
            term = jnp.dot(xs[:, columns], theirs[turn][...], preferred_element_type=F32)
            if turn == 0:
                acc[:, 256:512] = term
            else:
                acc[:, 256:512] += term

    @pl.when(step == pl.num_programs(0) - 1)
    def _():
        core = meta[0]
        factor = math.log2(math.e) / math.sqrt(HEAD)
        scale = factor * lax.rsqrt(jnp.sum(ss[...], axis=-1, keepdims=True) / WIDTH + 1e-05)
        for i, slot in enumerate(slots):
            at = slice(i * BLOCK, (i + 1) * BLOCK)
            c, s = angles_of(outer, inner, slot, meta)
            c = c * scale[at]
            s = s * scale[at]
            heads = []
            for h in range(4):
                t = acc[at, h * HEAD : (h + 1) * HEAD]
                heads.append((t * c + pltpu.roll(t, HEAD // 2, 1) * s).astype(BF))
            q[i, 0] = heads[0]
            q[i, 1] = heads[1]
            q[i, 2] = jnp.where(core == 0, heads[2], heads[3])
            q[i, 3] = jnp.where(core == 0, heads[3], heads[2])


def project(queries, after, meta, pieces, places, slots, gain, own, theirs):
    n = len(slots)
    rows = n * BLOCK
    depth = WIDTH // 2
    steps = WIDTH // depth
    outer, inner = tables()
    turn = lambda i, m: lax.rem(m[0] + i, 2)
    across = lambda i, m: (0, turn(i, m))
    zero = lambda k: lambda i, m: (0,) * k
    if queries:
        weights = [
            pl.BlockSpec((depth, 256), lambda i, m: (turn(i, m), 0)),
        ] + [pl.BlockSpec((depth // 2, 256), lambda i, m: (0, 0))] * 4
        shape = (n, 4, BLOCK, HEAD)
        scratch = [pltpu.VMEM((rows, depth), BF), pltpu.VMEM((rows, 512), F32)]
    else:
        weights = [
            pl.BlockSpec((64, depth), across),
            pl.BlockSpec((64, depth), across),
        ] + [pl.BlockSpec((depth // 4, 256), lambda i, m: (2, 0))] * 4
        shape = (2, rows, HEAD)
        scratch = [
            pltpu.VMEM((rows, depth), BF),
            pltpu.VMEM((256, depth), BF),
            pltpu.VMEM((rows, 256), F32),
        ]
    return pl.pallas_call(
        functools.partial(q_kernel if queries else kv_kernel, places, slots, len(after)),
        grid_spec=pltpu.PrefetchScalarGridSpec(
            num_scalar_prefetch=1,
            grid=(steps,),
            in_specs=[pl.BlockSpec((count, depth), across) for _, count in places]
            + [pl.BlockSpec((1, depth), across)]
            + weights
            + [pl.BlockSpec((2, 16, 1, HEAD), zero(4)), pl.BlockSpec((2, BLOCK, HEAD), zero(3))]
            + [pl.BlockSpec(memory_space=pl.ANY)] * len(after),
            out_specs=pl.BlockSpec(shape, zero(len(shape))),
            scratch_shapes=scratch + [pltpu.VMEM((rows, HEAD), F32)],
        ),
        out_shape=jax.ShapeDtypeStruct(shape, BF),
        compiler_params=pltpu.CompilerParams(vmem_limit_bytes=56 << 20),
        cost_estimate=pl.CostEstimate(
            flops=2 * rows * WIDTH * 512, bytes_accessed=2 * WIDTH * (rows + 512), transcendentals=0
        )
        if queries
        else TINY,
        name="queries" if queries else "keys",
    )(meta, *pieces, gain, *own, *theirs, outer, inner, *after)


def attend_kernel(slots, waits, meta, q, bits, kv_near, kv_far, their_near, their_far, *refs):
    wo, *theirs_wo = refs[:5]
    outs = refs[5 + waits : -3]
    heads, key, value = refs[-3:]
    nb = len(slots)
    for i, target in ((0, key), (1, value)):
        target[0:448] = kv_near[i]
        target[448:512] = kv_far[i]
        target[512:960] = their_near[i * 448 : (i + 1) * 448]
        target[960:1024] = their_far[i]
    z = meta[1]
    xh = meta[2]
    column = lax.broadcasted_iota(jnp.int32, (1, 1024), 1)
    mine = column < 512
    kblock = slot_block((column // BLOCK) % 8, z) * 2 + jnp.where(mine, xh, 1 - xh)
    kpos = kblock * BLOCK + column % BLOCK
    lane = lax.broadcasted_iota(jnp.int32, (HEAD, 1024), 0)
    hot = [(lane == kblock + h * 16).astype(BF) for h in range(2)]
    core = meta[0]
    for b in range(nb):
        block = slot_block(jnp.int32(slots[b]), z) * 2 + xh
        qpos = block * BLOCK + lax.broadcasted_iota(jnp.int32, (BLOCK, 1), 0)
        row = (lax.broadcasted_iota(jnp.int32, (8, 16), 1) == block).astype(BF)
        ours = jnp.dot(row, bits[...], preferred_element_type=F32).astype(BF)
        theirs = jnp.dot(row, their_near[896:912], preferred_element_type=F32).astype(BF)
        keep = [jnp.dot(ours, hot[h], preferred_element_type=F32)[0:1] for h in range(2)]
        pair = [jnp.dot(theirs, hot[h], preferred_element_type=F32)[0:1] for h in range(2)]
        keep.append(jnp.where(core == 0, pair[0], pair[1]))
        keep.append(jnp.where(core == 0, pair[1], pair[0]))
        bias = jnp.where(kpos <= qpos, 0.0, -1e30)
        s = lax.dot_general(
            q[slots[b]].reshape(256, HEAD),
            key[...],
            (((1,), (1,)), ((), ())),
            preferred_element_type=F32,
        )
        s = s.reshape(4, BLOCK, 1024) + bias[None]
        e = jnp.exp2(s - jnp.max(s, axis=-1, keepdims=True))
        total = jnp.sum(e, axis=-1, keepdims=True)
        p = jnp.concatenate([(e[h] * keep[h]).astype(BF) for h in range(4)], axis=0)
        o = jnp.dot(p, value[...], preferred_element_type=F32).reshape(4, BLOCK, HEAD)
        o = (o / (total * 0.9)).astype(BF)
        for h in range(4):
            heads[b * BLOCK : (b + 1) * BLOCK, h * HEAD : (h + 1) * HEAD] = o[h]
    x = heads[...]
    piece = 512
    for c in range(WIDTH // piece):
        cols = slice(c * piece, (c + 1) * piece)
        low = meta[3] == 0
        parts = [t[:, cols] for t in theirs_wo]
        w = jnp.concatenate(
            [
                wo[:, cols],
                jnp.where(low, parts[0], parts[1]),
                jnp.where(low, parts[1], parts[0]),
                jnp.where(low, parts[2], parts[3]),
                jnp.where(low, parts[3], parts[2]),
            ],
            axis=0,
        )
        t = jnp.dot(x, w, preferred_element_type=F32).astype(BF)
        half = c // (COLS // piece)
        at = slice(c * piece - half * COLS, (c + 1) * piece - half * COLS)
        for b in range(nb):
            outs[half * nb + b][:, at] = t[b * BLOCK : (b + 1) * BLOCK]


def attend(slots, after, meta, q, *rest):
    nb = len(slots)
    out_shape = [jax.ShapeDtypeStruct((BLOCK, COLS), BF)] * (2 * nb)
    vmem = pl.BlockSpec(memory_space=pltpu.VMEM)
    return pl.pallas_call(
        functools.partial(attend_kernel, slots, len(after)),
        in_specs=[pl.BlockSpec(memory_space=pltpu.SMEM), vmem]
        + [vmem] * 10
        + [pl.BlockSpec(memory_space=pl.ANY)] * len(after),
        out_specs=[vmem] * len(out_shape),
        out_shape=out_shape,
        scratch_shapes=[
            pltpu.VMEM((nb * BLOCK, 512), BF),
            pltpu.VMEM((1024, HEAD), BF),
            pltpu.VMEM((1024, HEAD), BF),
        ],
        compiler_params=pltpu.CompilerParams(vmem_limit_bytes=32 << 20),
        cost_estimate=TINY,
        name="attend",
    )(meta, q, *rest, *after)


def pick_kernel(meta, wq, kt, vt, wo, out, wo_out):
    quarter = WIDTH // 4
    wo_out[...] = wo[...]
    out[0:quarter] = wq[...]
    for i in range(quarter // 256):
        at = slice(i * 256, (i + 1) * 256)
        row = quarter + i * 128
        out[row : row + 64] = kt[:, at]
        out[row + 64 : row + 128] = vt[:, at]


def pick(meta, wq, kt, vt, wo):
    quarter = WIDTH // 4
    shapes = [(quarter + quarter // 2, 256), (BLOCK, WIDTH)]
    return pl.pallas_call(
        pick_kernel,
        grid_spec=pltpu.PrefetchScalarGridSpec(
            num_scalar_prefetch=1,
            grid=(1,),
            in_specs=[
                pl.BlockSpec((quarter, 256), lambda i, m: (2 * m[0] + m[3], 0)),
                pl.BlockSpec((64, quarter), lambda i, m: (0, 2 * m[0] + m[3])),
                pl.BlockSpec((64, quarter), lambda i, m: (0, 2 * m[0] + m[3])),
                pl.BlockSpec((BLOCK, WIDTH), lambda i, m: (2 * m[0] + m[3], 0)),
            ],
            out_specs=[pl.BlockSpec(shape, lambda i, m: (0, 0)) for shape in shapes],
        ),
        out_shape=[jax.ShapeDtypeStruct(shape, BF) for shape in shapes],
        compiler_params=pltpu.CompilerParams(vmem_limit_bytes=56 << 20),
        cost_estimate=TINY,
        name="pick",
    )(meta, wq, kt, vt, wo)


def gate_kernel(*refs):
    pass


def gate(arrays, after):
    n = len(arrays)
    anywhere = pl.BlockSpec(memory_space=pl.ANY)
    return pl.pallas_call(
        gate_kernel,
        in_specs=[anywhere] * (n + len(after)),
        out_specs=[anywhere] * n,
        out_shape=[jax.ShapeDtypeStruct(a.shape, a.dtype) for a in arrays],
        input_output_aliases={i: i for i in range(n)},
        cost_estimate=TINY,
        name="gate",
    )(*arrays, *after)


def from_x(array):
    return lax.ppermute(array, ("xl", "xh"), [(i, 3 - i) for i in range(4)])


def from_y(array):
    return lax.ppermute(array, "y", [(i, i ^ 1) for i in range(4)])


def from_core(array):
    return lax.ppermute(array, "c", [(0, 1), (1, 0)])


def pair(array):
    return lax.ppermute(array, "xh", [(0, 1), (1, 0)])


def add(a, b):
    return (a.astype(F32) + b.astype(F32)).astype(BF)


def on_device(
    layer_input, norm_gain, query_weight, key_weight, value_matrix, output_weight, keep_bits
):
    core = lax.axis_index("c")
    z = lax.axis_index("z")
    xh = lax.axis_index("xh")

    pieces = [layer_input]
    places = [(0, BLOCK)]
    r = layer_input
    l = layer_input
    for s in range(3):
        r = lax.ppermute(r, "z", RIGHT)
        l = lax.ppermute(l, "z", LEFT)
        pieces += [r, l]
        at = BLOCK * (1 + 2 * s)
        places += [(at, BLOCK), (at + BLOCK, BLOCK)]
        if s == 0:
            step_one = [r, l]
        if s == 1:
            step_two = [r, l]
    step_three = [r, l]
    last = [lax.ppermute(r[:HALF], "z", RIGHT), lax.ppermute(l[HALF:], "z", LEFT)]
    last_places = [(0, HALF), (HALF, HALF)]

    meta = jnp.stack([core, z, xh, lax.rem(lax.axis_index("y"), 2)]).astype(jnp.int32)
    kt = key_weight.T
    vt = value_matrix.T
    mine, wo_mine = pick(meta, query_weight, kt, vt, output_weight)
    got = from_x(mine)
    (got,) = gate([got], step_one)
    near_got = from_y(got)
    (wo_mine,) = gate([wo_mine], [step_two[0]])
    wo_got = from_x(wo_mine)
    (wo_got,) = gate([wo_got], step_three)
    wo_near_got = from_y(wo_got)
    (near_got,) = gate([near_got], step_three)
    theirs = [got, near_got, from_core(got), from_core(near_got)]

    bits = keep_bits.astype(BF).transpose(1, 0, 2).reshape(16, 32)
    bits = jnp.pad(bits, ((0, 0), (0, HEAD - 32)))

    gain = norm_gain[None, :]
    kv_near = project(False, [], meta, pieces, places, range(7), gain, (kt, vt), theirs)
    their_near = pair(jnp.concatenate([kv_near.reshape(896, HEAD), bits]))
    kv_far = project(False, [kv_near], meta, last, last_places, [7], gain, (kt, vt), theirs)
    their_far = pair(kv_far)
    everything = places + [(448 + start, count) for start, count in last_places]
    q = project(
        True, [kv_far], meta, pieces + last, everything, range(8), gain, (query_weight,), theirs
    )
    wo_got, wo_near_got = gate([wo_got, wo_near_got], [kv_far])
    shared = (bits, kv_near, kv_far, their_near, their_far, output_weight, wo_got, wo_near_got, from_core(wo_got), from_core(wo_near_got))

    near = {}

    def compute(slots, after):
        got = attend(slots, after, meta, q, *shared)
        for i, slot in enumerate(slots):
            near[(NEAR + [4])[slot]] = (got[i], got[len(slots) + i])
        return got

    block = lambda d, c: near[d][c]
    done = compute([7, 5, 6], [])
    compute([3, 4, 0, 1, 2], [done[0]])
    far = near[4]
    r = [lax.ppermute(far[0], "z", RIGHT), None]
    l = [None, lax.ppermute(far[1], "z", LEFT)]
    r = [add(r[0], block(3, 0)), block(3, 1)]
    l = [block(-3, 0), add(l[1], block(-3, 1))]
    for d in (2, 1):
        for c in range(2):
            r[c] = add(lax.ppermute(r[c], "z", RIGHT), block(d, c))
            l[c] = add(lax.ppermute(l[c], "z", LEFT), block(-d, c))
    total = []
    for c in range(2):
        right = lax.ppermute(r[c], "z", RIGHT)
        left = lax.ppermute(l[c], "z", LEFT)
        total.append(block(0, c).astype(F32) + right.astype(F32) + left.astype(F32))
    total = jnp.concatenate(total, axis=1)
    return (layer_input.astype(F32) + total).astype(BF)


def solution(mesh):
    split = Mesh(mesh.devices.reshape(2, 4, 2, Z, 2), ("xl", "y", "c", "z", "xh"))
    every = ("xl", "y", "c", "z", "xh")
    tensor = ("z", "xh")
    return jax.shard_map(
        on_device,
        mesh=split,
        in_specs=(
            P(every, None),
            P(),
            P(None, tensor),
            P(None, tensor),
            P(None, tensor),
            P(tensor, None),
            P(every, None, None),
        ),
        out_specs=P(every, None),
        check_vma=False,
    )
```

```python
import functools
import math

import jax
import jax.numpy as jnp
import numpy as np
from jax import lax
from jax.experimental import pallas as pl
from jax.experimental.pallas import tpu as pltpu
from jax.sharding import Mesh
from jax.sharding import PartitionSpec as P

HEAD = 128
BLOCK = 64
WIDTH = 4096
Z = 8
HALF = 32
COLS = 2048
THETA = 1000000.0
RIGHT = [(i, (i + 1) % Z) for i in range(Z)]
LEFT = [(i, (i - 1) % Z) for i in range(Z)]
NEAR = [0, -1, 1, -2, 2, -3, 3]
BF = jnp.bfloat16
F32 = jnp.float32
TINY = pl.CostEstimate(flops=1000, bytes_accessed=1000, transcendentals=0)


def slot_block(slot, z):
    offset = jnp.where(slot % 2 == 1, -((slot + 1) // 2), slot // 2)
    return lax.rem(z + offset + Z, Z)


def tables():
    freqs = THETA ** (-np.arange(HEAD // 2) * 2.0 / HEAD)

    def table(positions):
        angles = positions[:, None] * freqs[None, :]
        cosine, sine = np.cos(angles), np.sin(angles)
        return np.stack(
            [np.concatenate([cosine, cosine], 1), np.concatenate([-sine, sine], 1)]
        ).astype(np.float32)

    return table(np.arange(16) * float(BLOCK))[:, :, None, :], table(np.arange(BLOCK) * 1.0)


def load_tokens(places, pieces, gain, xs, ss, step):
    depth = xs.shape[1]
    g = gain[...]
    for ref, (start, count) in zip(pieces, places):
        x = ref[...].astype(F32)
        sq = x * x
        part = sq[:, :HEAD]
        for i in range(1, depth // HEAD):
            part = part + sq[:, i * HEAD : (i + 1) * HEAD]
        at = slice(start, start + count)
        ss[at] = jnp.where(step == 0, part, ss[at] + part)
        xs[at] = (x * g).astype(BF)


def angles_of(outer, inner, slot, meta):
    block = slot_block(jnp.int32(slot), meta[1]) * 2 + meta[2]
    co = outer[0, block]
    so = outer[1, block]
    return inner[0] * co - inner[1] * so, inner[1] * co + inner[0] * so


def gather_sum(acc, term, step):
    acc[...] = jnp.where(step == 0, term, acc[...] + term)


def kv_kernel(places, slots, waits, meta, *refs):
    n = len(places)
    pieces = refs[:n]
    gain, kt, vt = refs[n : n + 3]
    theirs = refs[n + 3 : n + 7]
    outer, inner = refs[n + 7 : n + 9]
    kv, xs, kvs, acc, ss = refs[n + 9 + waits :]
    step = pl.program_id(0)
    load_tokens(places, pieces, gain, xs, ss, step)
    kvs[0:64] = kt[...]
    kvs[128:192] = vt[...]
    quarter = WIDTH // 4
    for turn in range(2):

        @pl.when(step == turn)
        def _():
            for t, base in ((0, meta[3] * quarter), (1, (1 - meta[3]) * quarter)):
                part = theirs[2 * turn + t]
                for i in range(quarter // 256):
                    at = pl.ds(pl.multiple_of(base + i * 256, 256), 256)
                    kvs[64:128, at] = part[i * 128 : i * 128 + 64]
                    kvs[192:256, at] = part[i * 128 + 64 : i * 128 + 128]

    term = lax.dot_general(
        xs[...], kvs[...], (((1,), (1,)), ((), ())), preferred_element_type=F32
    )
    gather_sum(acc, term, step)

    @pl.when(step == pl.num_programs(0) - 1)
    def _():
        first = meta[2] == 0

        def ordered(t):
            return jnp.where(first, t, pltpu.roll(t, HEAD // 2, 1))

        scale = lax.rsqrt(jnp.sum(ss[...], axis=-1, keepdims=True) / WIDTH + 1e-05)
        kv[1] = ordered(acc[:, HEAD:] * scale).astype(BF)
        key = ordered(acc[:, :HEAD] * scale).astype(BF).astype(F32)
        turned = pltpu.roll(key, HEAD // 2, 1)
        for i, slot in enumerate(slots):
            at = slice(i * BLOCK, (i + 1) * BLOCK)
            c, s = angles_of(outer, inner, slot, meta)
            kv[0, at] = (key[at] * c + turned[at] * s).astype(BF)


def q_kernel(places, slots, waits, meta, *refs):
    n = len(places)
    pieces = refs[:n]
    gain, wq = refs[n : n + 2]
    theirs = refs[n + 2 : n + 6]
    outer, inner = refs[n + 6 : n + 8]
    q, xs, acc, ss = refs[n + 8 + waits :]
    step = pl.program_id(0)
    load_tokens(places, pieces, gain, xs, ss, step)
    x = xs[...]
    gather_sum(acc.at[:, 0:256], jnp.dot(x, wq[...], preferred_element_type=F32), step)
    for turn in range(4):

        @pl.when(step == turn // 2)
        def _():
            place = meta[3] if turn % 2 == 0 else 1 - meta[3]
            quarter = WIDTH // 4
            columns = pl.ds(pl.multiple_of(place * quarter, quarter), quarter)
            term = jnp.dot(xs[:, columns], theirs[turn][...], preferred_element_type=F32)
            if turn == 0:
                acc[:, 256:512] = term
            else:
                acc[:, 256:512] += term

    @pl.when(step == pl.num_programs(0) - 1)
    def _():
        core = meta[0]
        factor = math.log2(math.e) / math.sqrt(HEAD)
        scale = factor * lax.rsqrt(jnp.sum(ss[...], axis=-1, keepdims=True) / WIDTH + 1e-05)
        for i, slot in enumerate(slots):
            at = slice(i * BLOCK, (i + 1) * BLOCK)
            c, s = angles_of(outer, inner, slot, meta)
            c = c * scale[at]
            s = s * scale[at]
            heads = []
            for h in range(4):
                t = acc[at, h * HEAD : (h + 1) * HEAD]
                heads.append((t * c + pltpu.roll(t, HEAD // 2, 1) * s).astype(BF))
            q[i, 0] = heads[0]
            q[i, 1] = heads[1]
            q[i, 2] = jnp.where(core == 0, heads[2], heads[3])
            q[i, 3] = jnp.where(core == 0, heads[3], heads[2])


def project(queries, after, meta, pieces, places, slots, gain, own, theirs):
    n = len(slots)
    rows = n * BLOCK
    depth = WIDTH // 2
    steps = WIDTH // depth
    outer, inner = tables()
    turn = lambda i, m: lax.rem(m[0] + i, 2)
    across = lambda i, m: (0, turn(i, m))
    zero = lambda k: lambda i, m: (0,) * k
    if queries:
        weights = [
            pl.BlockSpec((depth, 256), lambda i, m: (turn(i, m), 0)),
        ] + [pl.BlockSpec((depth // 2, 256), lambda i, m: (0, 0))] * 4
        shape = (n, 4, BLOCK, HEAD)
        scratch = [pltpu.VMEM((rows, depth), BF), pltpu.VMEM((rows, 512), F32)]
    else:
        weights = [
            pl.BlockSpec((64, depth), across),
            pl.BlockSpec((64, depth), across),
        ] + [pl.BlockSpec((depth // 4, 256), lambda i, m: (2, 0))] * 4
        shape = (2, rows, HEAD)
        scratch = [
            pltpu.VMEM((rows, depth), BF),
            pltpu.VMEM((256, depth), BF),
            pltpu.VMEM((rows, 256), F32),
        ]
    return pl.pallas_call(
        functools.partial(q_kernel if queries else kv_kernel, places, slots, len(after)),
        grid_spec=pltpu.PrefetchScalarGridSpec(
            num_scalar_prefetch=1,
            grid=(steps,),
            in_specs=[pl.BlockSpec((count, depth), across) for _, count in places]
            + [pl.BlockSpec((1, depth), across)]
            + weights
            + [pl.BlockSpec((2, 16, 1, HEAD), zero(4)), pl.BlockSpec((2, BLOCK, HEAD), zero(3))]
            + [pl.BlockSpec(memory_space=pl.ANY)] * len(after),
            out_specs=pl.BlockSpec(shape, zero(len(shape))),
            scratch_shapes=scratch + [pltpu.VMEM((rows, HEAD), F32)],
        ),
        out_shape=jax.ShapeDtypeStruct(shape, BF),
        compiler_params=pltpu.CompilerParams(vmem_limit_bytes=(56 if queries else 40) << 20),
        cost_estimate=pl.CostEstimate(
            flops=2 * rows * WIDTH * 512, bytes_accessed=2 * WIDTH * (rows + 512), transcendentals=0
        )
        if queries
        else TINY,
        name="queries" if queries else "keys",
    )(meta, *pieces, gain, *own, *theirs, outer, inner, *after)


def attend_kernel(slots, waits, meta, q, bits, kv_near, kv_far, their_near, their_far, *refs):
    wo, *theirs_wo = refs[:5]
    outs = refs[5 + waits : -3]
    heads, key, value = refs[-3:]
    nb = len(slots)
    for i, target in ((0, key), (1, value)):
        target[0:448] = kv_near[i]
        target[448:512] = kv_far[i]
        target[512:960] = their_near[i * 448 : (i + 1) * 448]
        target[960:1024] = their_far[i]
    z = meta[1]
    xh = meta[2]
    column = lax.broadcasted_iota(jnp.int32, (1, 1024), 1)
    mine = column < 512
    kblock = slot_block((column // BLOCK) % 8, z) * 2 + jnp.where(mine, xh, 1 - xh)
    kpos = kblock * BLOCK + column % BLOCK
    lane = lax.broadcasted_iota(jnp.int32, (HEAD, 1024), 0)
    hot = [(lane == kblock + h * 16).astype(BF) for h in range(2)]
    core = meta[0]
    for b in range(nb):
        block = slot_block(jnp.int32(slots[b]), z) * 2 + xh
        qpos = block * BLOCK + lax.broadcasted_iota(jnp.int32, (BLOCK, 1), 0)
        row = (lax.broadcasted_iota(jnp.int32, (8, 16), 1) == block).astype(BF)
        ours = jnp.dot(row, bits[...], preferred_element_type=F32).astype(BF)
        theirs = jnp.dot(row, their_near[896:912], preferred_element_type=F32).astype(BF)
        keep = [jnp.dot(ours, hot[h], preferred_element_type=F32)[0:1] for h in range(2)]
        pair = [jnp.dot(theirs, hot[h], preferred_element_type=F32)[0:1] for h in range(2)]
        keep.append(jnp.where(core == 0, pair[0], pair[1]))
        keep.append(jnp.where(core == 0, pair[1], pair[0]))
        bias = jnp.where(kpos <= qpos, 0.0, -1e30)
        s = lax.dot_general(
            q[slots[b]].reshape(256, HEAD),
            key[...],
            (((1,), (1,)), ((), ())),
            preferred_element_type=F32,
        )
        s = s.reshape(4, BLOCK, 1024) + bias[None]
        e = jnp.exp2(s - jnp.max(s, axis=-1, keepdims=True))
        total = jnp.sum(e, axis=-1, keepdims=True)
        p = jnp.concatenate([(e[h] * keep[h]).astype(BF) for h in range(4)], axis=0)
        o = jnp.dot(p, value[...], preferred_element_type=F32).reshape(4, BLOCK, HEAD)
        o = (o / (total * 0.9)).astype(BF)
        for h in range(4):
            heads[b * BLOCK : (b + 1) * BLOCK, h * HEAD : (h + 1) * HEAD] = o[h]
    x = heads[...]
    piece = 512
    for c in range(WIDTH // piece):
        cols = slice(c * piece, (c + 1) * piece)
        low = meta[3] == 0
        parts = [t[:, cols] for t in theirs_wo]
        w = jnp.concatenate(
            [
                wo[:, cols],
                jnp.where(low, parts[0], parts[1]),
                jnp.where(low, parts[1], parts[0]),
                jnp.where(low, parts[2], parts[3]),
                jnp.where(low, parts[3], parts[2]),
            ],
            axis=0,
        )
        t = jnp.dot(x, w, preferred_element_type=F32).astype(BF)
        half = c // (COLS // piece)
        at = slice(c * piece - half * COLS, (c + 1) * piece - half * COLS)
        for b in range(nb):
            outs[half * nb + b][:, at] = t[b * BLOCK : (b + 1) * BLOCK]


def attend(slots, after, meta, q, *rest):
    nb = len(slots)
    out_shape = [jax.ShapeDtypeStruct((BLOCK, COLS), BF)] * (2 * nb)
    vmem = pl.BlockSpec(memory_space=pltpu.VMEM)
    return pl.pallas_call(
        functools.partial(attend_kernel, slots, len(after)),
        in_specs=[pl.BlockSpec(memory_space=pltpu.SMEM), vmem]
        + [vmem] * 10
        + [pl.BlockSpec(memory_space=pl.ANY)] * len(after),
        out_specs=[vmem] * len(out_shape),
        out_shape=out_shape,
        scratch_shapes=[
            pltpu.VMEM((nb * BLOCK, 512), BF),
            pltpu.VMEM((1024, HEAD), BF),
            pltpu.VMEM((1024, HEAD), BF),
        ],
        compiler_params=pltpu.CompilerParams(vmem_limit_bytes=32 << 20),
        cost_estimate=TINY,
        name="attend",
    )(meta, q, *rest, *after)


def pick_kernel(meta, wq, kt, vt, wo, out, wo_out):
    quarter = WIDTH // 4
    wo_out[...] = wo[...]
    out[0:quarter] = wq[...]
    for i in range(quarter // 256):
        at = slice(i * 256, (i + 1) * 256)
        row = quarter + i * 128
        out[row : row + 64] = kt[:, at]
        out[row + 64 : row + 128] = vt[:, at]


def pick(meta, wq, kt, vt, wo):
    quarter = WIDTH // 4
    shapes = [(quarter + quarter // 2, 256), (BLOCK, WIDTH)]
    return pl.pallas_call(
        pick_kernel,
        grid_spec=pltpu.PrefetchScalarGridSpec(
            num_scalar_prefetch=1,
            grid=(1,),
            in_specs=[
                pl.BlockSpec((quarter, 256), lambda i, m: (2 * m[0] + m[3], 0)),
                pl.BlockSpec((64, quarter), lambda i, m: (0, 2 * m[0] + m[3])),
                pl.BlockSpec((64, quarter), lambda i, m: (0, 2 * m[0] + m[3])),
                pl.BlockSpec((BLOCK, WIDTH), lambda i, m: (2 * m[0] + m[3], 0)),
            ],
            out_specs=[pl.BlockSpec(shape, lambda i, m: (0, 0)) for shape in shapes],
        ),
        out_shape=[jax.ShapeDtypeStruct(shape, BF) for shape in shapes],
        compiler_params=pltpu.CompilerParams(vmem_limit_bytes=56 << 20),
        cost_estimate=TINY,
        name="pick",
    )(meta, wq, kt, vt, wo)


def gate_kernel(*refs):
    pass


def gate(arrays, after):
    n = len(arrays)
    anywhere = pl.BlockSpec(memory_space=pl.ANY)
    return pl.pallas_call(
        gate_kernel,
        in_specs=[anywhere] * (n + len(after)),
        out_specs=[anywhere] * n,
        out_shape=[jax.ShapeDtypeStruct(a.shape, a.dtype) for a in arrays],
        input_output_aliases={i: i for i in range(n)},
        compiler_params=pltpu.CompilerParams(vmem_limit_bytes=1 << 20),
        cost_estimate=TINY,
        name="gate",
    )(*arrays, *after)


def from_x(array):
    return lax.ppermute(array, ("xl", "xh"), [(i, 3 - i) for i in range(4)])


def from_y(array):
    return lax.ppermute(array, "y", [(i, i ^ 1) for i in range(4)])


def from_core(array):
    return lax.ppermute(array, "c", [(0, 1), (1, 0)])


def pair(array):
    return lax.ppermute(array, "xh", [(0, 1), (1, 0)])


def add(a, b):
    return (a.astype(F32) + b.astype(F32)).astype(BF)


def on_device(
    layer_input, norm_gain, query_weight, key_weight, value_matrix, output_weight, keep_bits
):
    core = lax.axis_index("c")
    z = lax.axis_index("z")
    xh = lax.axis_index("xh")

    pieces = [layer_input]
    places = [(0, BLOCK)]
    r = layer_input
    l = layer_input
    for s in range(3):
        r = lax.ppermute(r, "z", RIGHT)
        l = lax.ppermute(l, "z", LEFT)
        pieces += [r, l]
        at = BLOCK * (1 + 2 * s)
        places += [(at, BLOCK), (at + BLOCK, BLOCK)]
        if s == 0:
            step_one = [r, l]
        if s == 1:
            step_two = [r, l]
    step_three = [r, l]
    last = [lax.ppermute(r[:HALF], "z", RIGHT), lax.ppermute(l[HALF:], "z", LEFT)]
    last_places = [(0, HALF), (HALF, HALF)]

    meta = jnp.stack([core, z, xh, lax.rem(lax.axis_index("y"), 2)]).astype(jnp.int32)
    kt = key_weight.T
    vt = value_matrix.T
    mine, wo_mine = pick(meta, query_weight, kt, vt, output_weight)
    got = from_x(mine)
    (got,) = gate([got], step_one)
    near_got = from_y(got)
    (wo_mine,) = gate([wo_mine], [step_two[0]])
    wo_got = from_x(wo_mine)
    (wo_got,) = gate([wo_got], step_three)
    wo_near_got = from_y(wo_got)
    (near_got,) = gate([near_got], step_three)
    theirs = [got, near_got, from_core(got), from_core(near_got)]

    bits = keep_bits.astype(BF).transpose(1, 0, 2).reshape(16, 32)
    bits = jnp.pad(bits, ((0, 0), (0, HEAD - 32)))

    gain = norm_gain[None, :]
    kv_near = project(False, [], meta, pieces, places, range(7), gain, (kt, vt), theirs)
    their_near = pair(jnp.concatenate([kv_near.reshape(896, HEAD), bits]))
    kv_far = project(False, [kv_near], meta, last, last_places, [7], gain, (kt, vt), theirs)
    their_far = pair(kv_far)
    everything = places + [(448 + start, count) for start, count in last_places]
    q = project(
        True, [kv_far], meta, pieces + last, everything, range(8), gain, (query_weight,), theirs
    )
    wo_got, wo_near_got = gate([wo_got, wo_near_got], [kv_far])
    shared = (bits, kv_near, kv_far, their_near, their_far, output_weight, wo_got, wo_near_got, from_core(wo_got), from_core(wo_near_got))

    near = {}

    def compute(slots, after):
        got = attend(slots, after, meta, q, *shared)
        for i, slot in enumerate(slots):
            near[(NEAR + [4])[slot]] = (got[i], got[len(slots) + i])
        return got

    block = lambda d, c: near[d][c]
    done = compute([7, 5, 6], [])
    compute([3, 4, 0, 1, 2], [done[0]])
    far = near[4]
    r = [lax.ppermute(far[0], "z", RIGHT), None]
    l = [None, lax.ppermute(far[1], "z", LEFT)]
    r = [add(r[0], block(3, 0)), block(3, 1)]
    l = [block(-3, 0), add(l[1], block(-3, 1))]
    for d in (2, 1):
        for c in range(2):
            r[c] = add(lax.ppermute(r[c], "z", RIGHT), block(d, c))
            l[c] = add(lax.ppermute(l[c], "z", LEFT), block(-d, c))
    total = []
    for c in range(2):
        right = lax.ppermute(r[c], "z", RIGHT)
        left = lax.ppermute(l[c], "z", LEFT)
        total.append(block(0, c).astype(F32) + right.astype(F32) + left.astype(F32))
    total = jnp.concatenate(total, axis=1)
    return (layer_input.astype(F32) + total).astype(BF)


def solution(mesh):
    split = Mesh(mesh.devices.reshape(2, 4, 2, Z, 2), ("xl", "y", "c", "z", "xh"))
    every = ("xl", "y", "c", "z", "xh")
    tensor = ("z", "xh")
    return jax.shard_map(
        on_device,
        mesh=split,
        in_specs=(
            P(every, None),
            P(),
            P(None, tensor),
            P(None, tensor),
            P(None, tensor),
            P(tensor, None),
            P(every, None, None),
        ),
        out_specs=P(every, None),
        check_vma=False,
    )
```

```python
import functools
import math

import jax
import jax.numpy as jnp
import numpy as np
from jax import lax
from jax.experimental import pallas as pl
from jax.experimental.pallas import tpu as pltpu
from jax.sharding import Mesh
from jax.sharding import PartitionSpec as P

HEAD = 128
BLOCK = 64
WIDTH = 4096
Z = 8
HALF = 32
COLS = 2048
THETA = 1000000.0
RIGHT = [(i, (i + 1) % Z) for i in range(Z)]
LEFT = [(i, (i - 1) % Z) for i in range(Z)]
NEAR = [0, -1, 1, -2, 2, -3, 3]
BF = jnp.bfloat16
F32 = jnp.float32
TINY = pl.CostEstimate(flops=1000, bytes_accessed=1000, transcendentals=0)


def slot_block(slot, z):
    offset = jnp.where(slot % 2 == 1, -((slot + 1) // 2), slot // 2)
    return lax.rem(z + offset + Z, Z)


def tables():
    freqs = THETA ** (-np.arange(HEAD // 2) * 2.0 / HEAD)

    def table(positions):
        angles = positions[:, None] * freqs[None, :]
        cosine, sine = np.cos(angles), np.sin(angles)
        return np.stack(
            [np.concatenate([cosine, cosine], 1), np.concatenate([-sine, sine], 1)]
        ).astype(np.float32)

    return table(np.arange(16) * float(BLOCK))[:, :, None, :], table(np.arange(BLOCK) * 1.0)


def load_tokens(places, pieces, gain, xs, ss, step):
    depth = xs.shape[1]
    g = gain[...]
    for ref, (start, count) in zip(pieces, places):
        x = ref[...].astype(F32)
        sq = x * x
        part = sq[:, :HEAD]
        for i in range(1, depth // HEAD):
            part = part + sq[:, i * HEAD : (i + 1) * HEAD]
        at = slice(start, start + count)
        ss[at] = jnp.where(step == 0, part, ss[at] + part)
        xs[at] = (x * g).astype(BF)


def angles_of(outer, inner, slot, meta):
    block = slot_block(jnp.int32(slot), meta[1]) * 2 + meta[2]
    co = outer[0, block]
    so = outer[1, block]
    return inner[0] * co - inner[1] * so, inner[1] * co + inner[0] * so


def gather_sum(acc, term, step):
    acc[...] = jnp.where(step == 0, term, acc[...] + term)


def kv_kernel(places, slots, waits, meta, *refs):
    n = len(places)
    pieces = refs[:n]
    gain, kt, vt = refs[n : n + 3]
    theirs = refs[n + 3 : n + 7]
    outer, inner = refs[n + 7 : n + 9]
    kv, xs, kvs, acc, ss = refs[n + 9 + waits :]
    step = pl.program_id(0)
    load_tokens(places, pieces, gain, xs, ss, step)
    kvs[0:64] = kt[...]
    kvs[128:192] = vt[...]
    quarter = WIDTH // 4
    for turn in range(2):

        @pl.when(step == turn)
        def _():
            for t, base in ((0, meta[3] * quarter), (1, (1 - meta[3]) * quarter)):
                part = theirs[2 * turn + t]
                for i in range(quarter // 256):
                    at = pl.ds(pl.multiple_of(base + i * 256, 256), 256)
                    kvs[64:128, at] = part[i * 128 : i * 128 + 64]
                    kvs[192:256, at] = part[i * 128 + 64 : i * 128 + 128]

    term = lax.dot_general(
        xs[...], kvs[...], (((1,), (1,)), ((), ())), preferred_element_type=F32
    )
    gather_sum(acc, term, step)

    @pl.when(step == pl.num_programs(0) - 1)
    def _():
        first = meta[2] == 0

        def ordered(t):
            return jnp.where(first, t, pltpu.roll(t, HEAD // 2, 1))

        scale = lax.rsqrt(jnp.sum(ss[...], axis=-1, keepdims=True) / WIDTH + 1e-05)
        kv[1] = ordered(acc[:, HEAD:] * scale).astype(BF)
        key = ordered(acc[:, :HEAD] * scale).astype(BF).astype(F32)
        turned = pltpu.roll(key, HEAD // 2, 1)
        for i, slot in enumerate(slots):
            at = slice(i * BLOCK, (i + 1) * BLOCK)
            c, s = angles_of(outer, inner, slot, meta)
            kv[0, at] = (key[at] * c + turned[at] * s).astype(BF)


def q_kernel(places, slots, waits, meta, *refs):
    n = len(places)
    pieces = refs[:n]
    gain, wq = refs[n : n + 2]
    theirs = refs[n + 2 : n + 6]
    outer, inner = refs[n + 6 : n + 8]
    q, xs, acc, ss = refs[n + 8 + waits :]
    step = pl.program_id(0)
    load_tokens(places, pieces, gain, xs, ss, step)
    x = xs[...]
    gather_sum(acc.at[:, 0:256], jnp.dot(x, wq[...], preferred_element_type=F32), step)
    for turn in range(4):

        @pl.when(step == turn // 2)
        def _():
            place = meta[3] if turn % 2 == 0 else 1 - meta[3]
            quarter = WIDTH // 4
            columns = pl.ds(pl.multiple_of(place * quarter, quarter), quarter)
            term = jnp.dot(xs[:, columns], theirs[turn][...], preferred_element_type=F32)
            if turn == 0:
                acc[:, 256:512] = term
            else:
                acc[:, 256:512] += term

    @pl.when(step == pl.num_programs(0) - 1)
    def _():
        core = meta[0]
        factor = math.log2(math.e) / math.sqrt(HEAD)
        scale = factor * lax.rsqrt(jnp.sum(ss[...], axis=-1, keepdims=True) / WIDTH + 1e-05)
        for i, slot in enumerate(slots):
            at = slice(i * BLOCK, (i + 1) * BLOCK)
            c, s = angles_of(outer, inner, slot, meta)
            c = c * scale[at]
            s = s * scale[at]
            heads = []
            for h in range(4):
                t = acc[at, h * HEAD : (h + 1) * HEAD]
                heads.append((t * c + pltpu.roll(t, HEAD // 2, 1) * s).astype(BF))
            q[i, 0] = heads[0]
            q[i, 1] = heads[1]
            q[i, 2] = jnp.where(core == 0, heads[2], heads[3])
            q[i, 3] = jnp.where(core == 0, heads[3], heads[2])


def project(queries, after, meta, pieces, places, slots, gain, own, theirs):
    n = len(slots)
    rows = n * BLOCK
    depth = WIDTH // 2
    steps = WIDTH // depth
    outer, inner = tables()
    turn = lambda i, m: lax.rem(m[0] + i, 2)
    across = lambda i, m: (0, turn(i, m))
    zero = lambda k: lambda i, m: (0,) * k
    if queries:
        weights = [
            pl.BlockSpec((depth, 256), lambda i, m: (turn(i, m), 0)),
        ] + [pl.BlockSpec((depth // 2, 256), lambda i, m: (0, 0))] * 4
        shape = (n, 4, BLOCK, HEAD)
        scratch = [pltpu.VMEM((rows, depth), BF), pltpu.VMEM((rows, 512), F32)]
    else:
        weights = [
            pl.BlockSpec((64, depth), across),
            pl.BlockSpec((64, depth), across),
        ] + [pl.BlockSpec((depth // 4, 256), lambda i, m: (2, 0))] * 4
        shape = (2, rows, HEAD)
        scratch = [
            pltpu.VMEM((rows, depth), BF),
            pltpu.VMEM((256, depth), BF),
            pltpu.VMEM((rows, 256), F32),
        ]
    return pl.pallas_call(
        functools.partial(q_kernel if queries else kv_kernel, places, slots, len(after)),
        grid_spec=pltpu.PrefetchScalarGridSpec(
            num_scalar_prefetch=1,
            grid=(steps,),
            in_specs=[pl.BlockSpec((count, depth), across) for _, count in places]
            + [pl.BlockSpec((1, depth), across)]
            + weights
            + [pl.BlockSpec((2, 16, 1, HEAD), zero(4)), pl.BlockSpec((2, BLOCK, HEAD), zero(3))]
            + [pl.BlockSpec(memory_space=pl.ANY)] * len(after),
            out_specs=pl.BlockSpec(shape, zero(len(shape))),
            scratch_shapes=scratch + [pltpu.VMEM((rows, HEAD), F32)],
        ),
        out_shape=jax.ShapeDtypeStruct(shape, BF),
        compiler_params=pltpu.CompilerParams(vmem_limit_bytes=(60 if queries else 40) << 20),
        cost_estimate=pl.CostEstimate(
            flops=2 * rows * WIDTH * 512, bytes_accessed=2 * WIDTH * (rows + 512), transcendentals=0
        )
        if queries
        else TINY,
        name="queries" if queries else "keys",
    )(meta, *pieces, gain, *own, *theirs, outer, inner, *after)


def attend_kernel(slots, waits, meta, q, bits, kv_near, kv_far, their_near, their_far, *refs):
    wo, *theirs_wo = refs[:5]
    outs = refs[5 + waits : -3]
    heads, key, value = refs[-3:]
    nb = len(slots)
    for i, target in ((0, key), (1, value)):
        target[0:448] = kv_near[i]
        target[448:512] = kv_far[i]
        target[512:960] = their_near[i * 448 : (i + 1) * 448]
        target[960:1024] = their_far[i]
    z = meta[1]
    xh = meta[2]
    column = lax.broadcasted_iota(jnp.int32, (1, 1024), 1)
    mine = column < 512
    kblock = slot_block((column // BLOCK) % 8, z) * 2 + jnp.where(mine, xh, 1 - xh)
    kpos = kblock * BLOCK + column % BLOCK
    lane = lax.broadcasted_iota(jnp.int32, (HEAD, 1024), 0)
    hot = [(lane == kblock + h * 16).astype(BF) for h in range(2)]
    core = meta[0]
    for b in range(nb):
        block = slot_block(jnp.int32(slots[b]), z) * 2 + xh
        qpos = block * BLOCK + lax.broadcasted_iota(jnp.int32, (BLOCK, 1), 0)
        row = (lax.broadcasted_iota(jnp.int32, (8, 16), 1) == block).astype(BF)
        ours = jnp.dot(row, bits[...], preferred_element_type=F32).astype(BF)
        theirs = jnp.dot(row, their_near[896:912], preferred_element_type=F32).astype(BF)
        keep = [jnp.dot(ours, hot[h], preferred_element_type=F32)[0:1] for h in range(2)]
        pair = [jnp.dot(theirs, hot[h], preferred_element_type=F32)[0:1] for h in range(2)]
        keep.append(jnp.where(core == 0, pair[0], pair[1]))
        keep.append(jnp.where(core == 0, pair[1], pair[0]))
        bias = jnp.where(kpos <= qpos, 0.0, -1e30)
        s = lax.dot_general(
            q[slots[b]].reshape(256, HEAD),
            key[...],
            (((1,), (1,)), ((), ())),
            preferred_element_type=F32,
        )
        s = s.reshape(4, BLOCK, 1024) + bias[None]
        e = jnp.exp2(s - jnp.max(s, axis=-1, keepdims=True))
        total = jnp.sum(e, axis=-1, keepdims=True)
        p = jnp.concatenate([(e[h] * keep[h]).astype(BF) for h in range(4)], axis=0)
        o = jnp.dot(p, value[...], preferred_element_type=F32).reshape(4, BLOCK, HEAD)
        o = (o / (total * 0.9)).astype(BF)
        for h in range(4):
            heads[b * BLOCK : (b + 1) * BLOCK, h * HEAD : (h + 1) * HEAD] = o[h]
    x = heads[...]
    piece = 512
    for c in range(WIDTH // piece):
        cols = slice(c * piece, (c + 1) * piece)
        low = meta[3] == 0
        parts = [t[:, cols] for t in theirs_wo]
        w = jnp.concatenate(
            [
                wo[:, cols],
                jnp.where(low, parts[0], parts[1]),
                jnp.where(low, parts[1], parts[0]),
                jnp.where(low, parts[2], parts[3]),
                jnp.where(low, parts[3], parts[2]),
            ],
            axis=0,
        )
        t = jnp.dot(x, w, preferred_element_type=F32).astype(BF)
        half = c // (COLS // piece)
        at = slice(c * piece - half * COLS, (c + 1) * piece - half * COLS)
        for b in range(nb):
            outs[half * nb + b][:, at] = t[b * BLOCK : (b + 1) * BLOCK]


def attend(slots, after, meta, q, *rest):
    nb = len(slots)
    out_shape = [jax.ShapeDtypeStruct((BLOCK, COLS), BF)] * (2 * nb)
    vmem = pl.BlockSpec(memory_space=pltpu.VMEM)
    return pl.pallas_call(
        functools.partial(attend_kernel, slots, len(after)),
        in_specs=[pl.BlockSpec(memory_space=pltpu.SMEM), vmem]
        + [vmem] * 10
        + [pl.BlockSpec(memory_space=pl.ANY)] * len(after),
        out_specs=[vmem] * len(out_shape),
        out_shape=out_shape,
        scratch_shapes=[
            pltpu.VMEM((nb * BLOCK, 512), BF),
            pltpu.VMEM((1024, HEAD), BF),
            pltpu.VMEM((1024, HEAD), BF),
        ],
        compiler_params=pltpu.CompilerParams(vmem_limit_bytes=32 << 20),
        cost_estimate=TINY,
        name="attend",
    )(meta, q, *rest, *after)


def pick_kernel(meta, wq, kt, vt, wo, out, wo_out):
    quarter = WIDTH // 4
    wo_out[...] = wo[...]
    out[0:quarter] = wq[...]
    for i in range(quarter // 256):
        at = slice(i * 256, (i + 1) * 256)
        row = quarter + i * 128
        out[row : row + 64] = kt[:, at]
        out[row + 64 : row + 128] = vt[:, at]


def pick(meta, wq, kt, vt, wo):
    quarter = WIDTH // 4
    shapes = [(quarter + quarter // 2, 256), (BLOCK, WIDTH)]
    return pl.pallas_call(
        pick_kernel,
        grid_spec=pltpu.PrefetchScalarGridSpec(
            num_scalar_prefetch=1,
            grid=(1,),
            in_specs=[
                pl.BlockSpec((quarter, 256), lambda i, m: (2 * m[0] + m[3], 0)),
                pl.BlockSpec((64, quarter), lambda i, m: (0, 2 * m[0] + m[3])),
                pl.BlockSpec((64, quarter), lambda i, m: (0, 2 * m[0] + m[3])),
                pl.BlockSpec((BLOCK, WIDTH), lambda i, m: (2 * m[0] + m[3], 0)),
            ],
            out_specs=[pl.BlockSpec(shape, lambda i, m: (0, 0)) for shape in shapes],
        ),
        out_shape=[jax.ShapeDtypeStruct(shape, BF) for shape in shapes],
        compiler_params=pltpu.CompilerParams(vmem_limit_bytes=56 << 20),
        cost_estimate=TINY,
        name="pick",
    )(meta, wq, kt, vt, wo)


def gate_kernel(*refs):
    pass


def gate(arrays, after):
    n = len(arrays)
    anywhere = pl.BlockSpec(memory_space=pl.ANY)
    return pl.pallas_call(
        gate_kernel,
        in_specs=[anywhere] * (n + len(after)),
        out_specs=[anywhere] * n,
        out_shape=[jax.ShapeDtypeStruct(a.shape, a.dtype) for a in arrays],
        input_output_aliases={i: i for i in range(n)},
        compiler_params=pltpu.CompilerParams(vmem_limit_bytes=1 << 20),
        cost_estimate=TINY,
        name="gate",
    )(*arrays, *after)


def from_x(array):
    return lax.ppermute(array, ("xl", "xh"), [(i, 3 - i) for i in range(4)])


def from_y(array):
    return lax.ppermute(array, "y", [(i, i ^ 1) for i in range(4)])


def from_core(array):
    return lax.ppermute(array, "c", [(0, 1), (1, 0)])


def pair(array):
    return lax.ppermute(array, "xh", [(0, 1), (1, 0)])


def add(a, b):
    return (a.astype(F32) + b.astype(F32)).astype(BF)


def on_device(
    layer_input, norm_gain, query_weight, key_weight, value_matrix, output_weight, keep_bits
):
    core = lax.axis_index("c")
    z = lax.axis_index("z")
    xh = lax.axis_index("xh")

    pieces = [layer_input]
    places = [(0, BLOCK)]
    r = layer_input
    l = layer_input
    for s in range(3):
        r = lax.ppermute(r, "z", RIGHT)
        l = lax.ppermute(l, "z", LEFT)
        pieces += [r, l]
        at = BLOCK * (1 + 2 * s)
        places += [(at, BLOCK), (at + BLOCK, BLOCK)]
        if s == 0:
            step_one = [r, l]
        if s == 1:
            step_two = [r, l]
    step_three = [r, l]
    last = [lax.ppermute(r[:HALF], "z", RIGHT), lax.ppermute(l[HALF:], "z", LEFT)]
    last_places = [(0, HALF), (HALF, HALF)]

    meta = jnp.stack([core, z, xh, lax.rem(lax.axis_index("y"), 2)]).astype(jnp.int32)
    kt = key_weight.T
    vt = value_matrix.T
    mine, wo_mine = pick(meta, query_weight, kt, vt, output_weight)
    got = from_x(mine)
    (got,) = gate([got], step_one)
    near_got = from_y(got)
    (wo_mine,) = gate([wo_mine], [step_two[0]])
    wo_got = from_x(wo_mine)
    (wo_got,) = gate([wo_got], step_three)
    wo_near_got = from_y(wo_got)
    (near_got,) = gate([near_got], step_three)
    theirs = [got, near_got, from_core(got), from_core(near_got)]

    bits = keep_bits.astype(BF).transpose(1, 0, 2).reshape(16, 32)
    bits = jnp.pad(bits, ((0, 0), (0, HEAD - 32)))

    gain = norm_gain[None, :]
    kv_near = project(False, [], meta, pieces, places, range(7), gain, (kt, vt), theirs)
    their_near = pair(jnp.concatenate([kv_near.reshape(896, HEAD), bits]))
    kv_far = project(False, [kv_near], meta, last, last_places, [7], gain, (kt, vt), theirs)
    their_far = pair(kv_far)
    everything = places + [(448 + start, count) for start, count in last_places]
    q = project(
        True, [kv_far], meta, pieces + last, everything, range(8), gain, (query_weight,), theirs
    )
    wo_got, wo_near_got = gate([wo_got, wo_near_got], [kv_far])
    shared = (bits, kv_near, kv_far, their_near, their_far, output_weight, wo_got, wo_near_got, from_core(wo_got), from_core(wo_near_got))

    near = {}

    def compute(slots, after):
        got = attend(slots, after, meta, q, *shared)
        for i, slot in enumerate(slots):
            near[(NEAR + [4])[slot]] = (got[i], got[len(slots) + i])
        return got

    block = lambda d, c: near[d][c]
    done = compute([7, 5, 6], [])
    compute([3, 4, 0, 1, 2], [done[0]])
    far = near[4]
    r = [lax.ppermute(far[0], "z", RIGHT), None]
    l = [None, lax.ppermute(far[1], "z", LEFT)]
    r = [add(r[0], block(3, 0)), block(3, 1)]
    l = [block(-3, 0), add(l[1], block(-3, 1))]
    for d in (2, 1):
        for c in range(2):
            r[c] = add(lax.ppermute(r[c], "z", RIGHT), block(d, c))
            l[c] = add(lax.ppermute(l[c], "z", LEFT), block(-d, c))
    total = []
    for c in range(2):
        right = lax.ppermute(r[c], "z", RIGHT)
        left = lax.ppermute(l[c], "z", LEFT)
        total.append(block(0, c).astype(F32) + right.astype(F32) + left.astype(F32))
    total = jnp.concatenate(total, axis=1)
    return (layer_input.astype(F32) + total).astype(BF)


def solution(mesh):
    split = Mesh(mesh.devices.reshape(2, 4, 2, Z, 2), ("xl", "y", "c", "z", "xh"))
    every = ("xl", "y", "c", "z", "xh")
    tensor = ("z", "xh")
    return jax.shard_map(
        on_device,
        mesh=split,
        in_specs=(
            P(every, None),
            P(),
            P(None, tensor),
            P(None, tensor),
            P(None, tensor),
            P(tensor, None),
            P(every, None, None),
        ),
        out_specs=P(every, None),
        check_vma=False,
    )
```
